256 devices in a mesh: cpty: 8 (over z_hi, x), path: 32 (over y, z_lo, core).
Axes of the slice: x: 4, y: 4, z: 8 (z_hi: 2, z_lo: 4; z = z_hi * 4 + z_lo), core: 2. Of those that a mesh axis runs over, the one named last changes fastest.
Arguments:
- exposures: bfloat16 [32768, 8, 4096], P('cpty', None, 'path'), may hold values from 0.099609375 to 2
- defaults: int32 [32768, 4096], P('cpty', 'path'), may hold values from 0 to 8
- base_rate: float32 [32768], P('cpty'), may hold values from 0.05 to 0.6
- loadings: bfloat16 [32768, 64], P('cpty'), may hold values from -1 to 1
- factors: bfloat16 [8, 64, 4096], P(None, None, 'path'), may hold values from -5 to 5
- weights: float32 [8], replicated, may hold values from 0.5 to 1.5
Outputs:
- value: float32 [], replicated
- loading_grad: float32 [32768, 64], P('cpty')
- factor_grad: float32 [8, 64, 4096], P(None, 'cpty', 'path')
The draws below stay inside these ranges and needn't reach their ends.
All inputs are finite; a program needn't handle non-finite values.
Results may differ from the reference program's by a relative error of at most 0.00045.
Values sent between devices are 32-bit elements; how exact they have to be, the bound alone decides.
A program may use at most 128 MiB of HBM per device.

```python
import math
import jax
import jax.numpy as jnp
from jax import lax

F = 64
W = 8
COUNTERPARTIES = 32768
PATHS = 4096


def touch_ends(drawn, stream_key, least, largest):
    extent = drawn.shape
    place = [jax.random.randint(jax.random.fold_in(stream_key, axis), (), 0, extent[axis]) for axis in range(len(extent))]
    drawn = drawn.at[tuple(place)].set(least)
    longest = extent.index(max(extent))
    place[longest] = (place[longest] + 1) % extent[longest]
    return drawn.at[tuple(place)].set(largest)


def raised(array, key, source, target, blocks, factor):
    owner, partner = [(jnp.arange(array.shape[dim]) // (array.shape[dim] // blocks)).reshape([-1 if axis == dim else 1 for axis in range(array.ndim)]) for dim in (source, target)]
    chosen = jax.random.permutation(key, blocks)[partner]
    strong = (owner == chosen) | (owner == (partner + blocks // 2) % blocks)
    return jnp.where(strong, factor * array, array)


def level_of(own_key, shape, shards, low, high):
    level, own = 1.0, jax.random.fold_in(own_key, 6)
    for dim, blocks in shards:
        draws = jnp.exp(jax.random.uniform(jax.random.fold_in(own, dim), (blocks,), jnp.float32, low / len(shards), high / len(shards)))
        level = level * jnp.repeat(draws, shape[dim] // blocks).reshape([-1 if axis == dim else 1 for axis in range(len(shape))])
    return level


def noise(key, shape, deviation, most, pieces=(), held_as=jnp.bfloat16):
    loudness = level_of(key, shape, pieces, -0.22, 0.18) if pieces else 1.0
    array = jax.random.normal(key, shape, jnp.float32) * deviation * loudness
    return jnp.minimum(jnp.maximum(array, -most), most).astype(held_as)


def noise_with(stream_key, shape, width, limit, pieces, heavy, kind=jnp.bfloat16):
    result = width * jax.random.normal(stream_key, shape, jnp.float32)
    if pieces:
        result = result * level_of(stream_key, shape, pieces, -0.22, 0.18)
    return jnp.clip(raised(result, jax.random.fold_in(stream_key, 3), *heavy), -limit, limit).astype(kind)


def setup_inputs(seed: int = 0) -> dict:
    keys = jax.random.split(jax.random.key(seed), 7)
    exposures = jnp.clip(0.099609375 + 1.9003906 * jax.random.uniform(keys[0], (COUNTERPARTIES, W, PATHS), jnp.float32) ** level_of(keys[0], (COUNTERPARTIES, W, PATHS), ((0, 8), (2, 32)), -0.2, 0.2), 0.099609375, 2.0).astype(jnp.bfloat16)
    defaults = touch_ends(jax.random.randint(keys[1], (COUNTERPARTIES, PATHS), 0, W + 1), jax.random.fold_in(keys[1], 1), 0, W).astype(jnp.int32)
    base_rate = jnp.clip(jnp.exp(math.log(0.6) - 2.4849067 * jax.random.uniform(keys[2], (COUNTERPARTIES,), jnp.float32) ** level_of(keys[2], (COUNTERPARTIES,), ((0, 8),), -0.2, 0.2)), 0.05, 0.6)
    loadings = noise_with(keys[3], (COUNTERPARTIES, F), F ** -0.5, 1.0, ((0, 8),), (0, 1, 8, 2.0))
    factors = noise(keys[4], (W, F, PATHS), 1.0, 5.0, ((2, 32),))
    weights = jnp.clip(jax.random.uniform(keys[5], (W,), jnp.float32, 0.5, 1.5), 0.5, 1.5)
    return {"exposures": exposures, "defaults": defaults, "base_rate": base_rate, "loadings": loadings, "factors": factors, "weights": weights}


dt_step = 0.5


def block_terms(loads, exposures, defaults, base_rate, factors, weights):
    x = jnp.einsum("cf,tfp->ctp", loads.astype(jnp.float32), factors.astype(jnp.float32))
    rate = base_rate[:, None, None] * jnp.exp(x)
    hazard = dt_step * jnp.cumsum(rate, axis=1)
    survival = jnp.exp(-hazard)
    dates = jnp.arange(W, dtype=jnp.int32)
    live = (dates[None, :, None] < defaults[:, None, :]).astype(jnp.float32)
    amount = weights[None, :, None] * live * exposures.astype(jnp.float32)
    weighted = amount * survival
    total = jnp.sum(weighted)
    grad_rate = -dt_step * jnp.flip(jnp.cumsum(jnp.flip(weighted, 1), axis=1), 1)
    grad_x = (rate * grad_rate).astype(jnp.bfloat16)
    loads_part = jnp.einsum("ctp,tfp->cf", grad_x.astype(jnp.float32), factors.astype(jnp.float32))
    factor_part = jnp.einsum("cf,ctp->tfp", loads.astype(jnp.float32), grad_x.astype(jnp.float32))
    return total, loads_part, factor_part


def reference(exposures, defaults, base_rate, loadings, factors, weights):
    block = math.gcd(COUNTERPARTIES, 512)
    count = COUNTERPARTIES // block
    exp_blocks = exposures.reshape(count, block, W, PATHS)
    def_blocks = defaults.reshape(count, block, PATHS)
    rate_blocks = base_rate.reshape(count, block)
    load_blocks = loadings.reshape(count, block, F)

    def step(carry, items):
        total, factor_sum = carry
        part_total, loads_part, factor_part = block_terms(items[3], items[0], items[1], items[2], factors, weights)
        return (total + part_total, factor_sum + factor_part), loads_part

    start = (jnp.zeros((), jnp.float32), jnp.zeros((W, F, PATHS), jnp.float32))
    (total, factor_sum), loads_parts = lax.scan(step, start, (exp_blocks, def_blocks, rate_blocks, load_blocks))
    value = total / (COUNTERPARTIES * PATHS)
    loading_grad = loads_parts.reshape(COUNTERPARTIES, F) / PATHS
    factor_grad = factor_sum * (F / COUNTERPARTIES)
    return value, loading_grad, factor_grad
```

```python
import functools
import math

import jax
import jax.numpy as jnp
from jax import lax
from jax.experimental import pallas as pl
from jax.experimental.pallas import tpu as pltpu
from jax.sharding import PartitionSpec as P

LOG2E = 1.4426950408889634
F32, BF = jnp.float32, jnp.bfloat16
MESH = pl.DeviceIdType.MESH
V = pltpu.VMEM


def split3(v):
    h = v.astype(BF)
    r = v - h.astype(F32)
    m = r.astype(BF)
    return h, m, (r - m.astype(F32)).astype(BF)


def terms(R, RB, NDMA, e_hbm, d_hbm, b_hbm, lt_hbm, f_hbm, w_ref, lg_ref, fp_ref, v_ref,
          e, d, bv, lt, f, f3, f2, ya, yb, ga, gb, fp, lg, dsem, ssem):
    CT = 4096
    NB = CT // R
    CH = CT // NDMA
    small = [pltpu.make_async_copy(f_hbm, f, ssem.at[0]), pltpu.make_async_copy(lt_hbm, lt, ssem.at[1]),
             pltpu.make_async_copy(b_hbm, bv, ssem.at[2])]
    for c in small:
        c.start()

    def chunk(i):
        s = pl.ds(i * CH, CH)
        return (pltpu.make_async_copy(e_hbm.at[s], e.at[s], dsem.at[0, i]),
                pltpu.make_async_copy(d_hbm.at[s], d.at[s], dsem.at[1, i]))

    for i in range(NDMA):
        for c in chunk(i):
            c.start()
    for c in small:
        c.wait()
    f3[...] = jnp.zeros_like(f3)
    for t in range(8):
        h, m, l = split3(f[t].astype(F32) * LOG2E)
        sl = slice(t * 128, (t + 1) * 128)
        f3[0:64, sl] = h
        f3[128:192, sl] = m
        f3[192:256, sl] = l
        f2[:, sl] = f[t]
    row = lax.broadcasted_iota(jnp.int32, (16, 1024), 0)
    f3[64:80, :] = jnp.where(row < 3, 1.0, 0.0).astype(BF)
    fp[...] = jnp.zeros_like(fp)
    v_ref[...] = jnp.zeros_like(v_ref)
    gb[...] = jnp.zeros_like(gb)
    wneg = [-math.log(2.0) * w_ref[t] for t in range(8)]

    def ydot(j, y):
        cs = pl.ds(pl.multiple_of(j * R, R), R)
        l = lt[:, cs]
        h, m, lo = split3(jnp.log2(bv[:, cs] * (0.5 * LOG2E)))
        row = lax.broadcasted_iota(jnp.int32, (16, R), 0)
        extra = jnp.where(row == 0, h.astype(F32), jnp.where(row == 1, m.astype(F32), jnp.where(row == 2, lo.astype(F32), 0.0))).astype(BF)
        l3 = jnp.concatenate([l, extra, jnp.zeros((48, R), BF), l, l], axis=0)
        y[...] = lax.dot_general(l3, f3[...], (((0,), (0,)), ((), ())), preferred_element_type=F32)

    def elem(j, y, gx):
        acc = None
        for q in range(R // RB):
            r = pl.multiple_of(j * R + q * RB, RB)
            rl = slice(q * RB, (q + 1) * RB)
            dd = d[pl.ds(r, RB), :]
            es = jnp.swapaxes(e[pl.ds(r, RB)], 0, 1).astype(F32)
            rates, wt, hz = [], [], None
            for t in range(8):
                rt = jnp.exp2(y[rl, t * 128:(t + 1) * 128])
                hz = -rt if t == 0 else hz - rt
                s = jnp.exp2(hz)
                a = jnp.where(t < dd, es[t], 0.0) * wneg[t]
                rates.append(rt)
                wt.append(a * s)
            g = None
            for t in range(7, -1, -1):
                g = wt[t] if g is None else g + wt[t]
                gx[rl, t * 128:(t + 1) * 128] = (rates[t] * g).astype(BF)
            for k in range(RB // 8):
                part = g[k * 8:(k + 1) * 8]
                acc = part if acc is None else acc + part
        v_ref[...] += acc

    def de(j, gx):
        cs = pl.ds(pl.multiple_of(j * R, R), R)
        g = gx[...]
        fp[...] += lax.dot_general(lt[:, cs], g, (((1,), (0,)), ((), ())), preferred_element_type=F32)
        lg[:, cs] = lax.dot_general(f2[...], g, (((1,), (1,)), ((), ())), preferred_element_type=F32)

    ydot(0, ya)
    per = CH // (2 * R)

    def body(k, _):
        @pl.when(k % per == 0)
        def _():
            for c in chunk(k // per):
                c.wait()
        j = 2 * k
        ydot(j + 1, yb)
        elem(j, ya, ga)
        de(jnp.maximum(j - 1, 0), gb)
        ydot(jnp.minimum(j + 2, NB - 1), ya)
        elem(j + 1, yb, gb)
        de(j, ga)
        return 0

    lax.fori_loop(0, NB // 2, body, 0)
    de(NB - 1, gb)
    oc = [pltpu.make_async_copy(lg, lg_ref, ssem.at[0]), pltpu.make_async_copy(fp, fp_ref, ssem.at[1])]
    for c in oc:
        c.start()
    for c in oc:
        c.wait()


def own_terms(exposures, defaults, base, lt, factors, weights):
    R, RB, NDMA, CT = 256, 32, 8, 4096
    A = pl.BlockSpec(memory_space=pl.ANY)
    return pl.pallas_call(
        functools.partial(terms, R, RB, NDMA),
        in_specs=[A, A, A, A, A, pl.BlockSpec(memory_space=pltpu.SMEM)],
        out_specs=[A, A, pl.BlockSpec(memory_space=V)],
        out_shape=[jax.ShapeDtypeStruct((64, CT), F32), jax.ShapeDtypeStruct((64, 1024), F32), jax.ShapeDtypeStruct((8, 128), F32)],
        scratch_shapes=[V((CT, 8, 128), BF), V((CT, 128), jnp.int32), V((1, CT), F32), V((64, CT), BF), V((8, 64, 128), BF),
                        V((256, 1024), BF), V((64, 1024), BF), V((R, 1024), F32), V((R, 1024), F32), V((R, 1024), BF), V((R, 1024), BF),
                        V((64, 1024), F32), V((64, CT), F32), pltpu.SemaphoreType.DMA((2, NDMA)), pltpu.SemaphoreType.DMA((3,))],
        compiler_params=pltpu.CompilerParams(vmem_limit_bytes=48 << 20),
    )(exposures, defaults, base, lt, factors, weights)


def sums(NCH, scale_l, scale_f, scale_v, lg, fp, vin, lo_ref, fo_ref, vo_ref,
         cbuf, rbuf, out, fbuf, vc, vbuf, vp, wbuf, tot, s_c, r_c, s_r, r_r, s_a, r_a, s_d, r_d, s_f, r_f, s_v, r_v, s_w, r_w, lsem):
    CW = 4096 // NCH
    Q = CW // 4
    ci, pi = lax.axis_index("cpty"), lax.axis_index("path")
    y, z, k = pi // 8, (pi // 2) % 4, pi % 2
    mate = (ci, pi - k + (1 - k))

    def chip(j):
        yy, zz = (y + j // 4) % 4, (z + j % 4) % 4
        return yy, zz, (ci, yy * 8 + zz * 2 + k)

    def fam(j):
        cc = (ci + j) % 8
        return cc, (cc, pi)

    barrier = pltpu.get_barrier_semaphore()
    for dev in [mate] + [chip(j)[2] for j in range(1, 16)] + [fam(j)[1] for j in range(1, 8)]:
        pl.semaphore_signal(barrier, inc=1, device_id=dev, device_id_type=MESH)
    pl.semaphore_wait(barrier, 23)

    def rc(src, dst, ss, rs, dev):
        return pltpu.make_async_remote_copy(src, dst, ss, rs, device_id=dev, device_id_type=MESH)

    mine = pl.multiple_of(k * 32, 32)
    other = pl.multiple_of(32 - k * 32, 32)

    def cc(i):
        return rc(lg.at[pl.ds(other, 32), pl.ds(i * CW, CW)], cbuf.at[i], s_c.at[i], r_c.at[i], mate)

    def rs(i, j):
        yy, zz, dev = chip(j)
        return rc(cbuf.at[i, pl.ds(pl.multiple_of(yy * 8, 8), 8), pl.ds(pl.multiple_of(zz * Q, Q), Q)], rbuf.at[i, j],
                  s_r.at[i, j], r_r.at[i, j], dev)

    def ag(i, j):
        _, _, dev = chip(j)
        piece = out.at[pl.ds(pl.multiple_of(mine + y * 8, 8), 8), pl.ds(pl.multiple_of(i * CW + z * Q, Q), Q)]
        return rc(piece, piece, s_a.at[i, j], r_a.at[i, j], dev)

    def dd(i):
        half = out.at[pl.ds(mine, 32), pl.ds(i * CW, CW)]
        return rc(half, half, s_d.at[i], r_d.at[i], mate)

    def ff(j):
        cc_, dev = fam(j)
        return rc(fp.at[pl.ds(pl.multiple_of(cc_ * 8, 8), 8)], fbuf.at[j], s_f.at[j], r_f.at[j], dev)

    vcopy = rc(vin, vc, s_v.at[0], r_v.at[0], mate)

    def vv(j):
        return rc(vp, vbuf.at[y * 4 + z], s_v.at[j], r_v.at[j], chip(j)[2])

    def ww(j):
        return rc(tot, wbuf.at[ci], s_w.at[j], r_w.at[j], fam(j)[1])

    vcopy.start()
    for i in range(NCH):
        cc(i).start()
    for j in range(1, 8):
        ff(j).start()
    vcopy.wait_recv()
    vp[...] = vin[...] + vc[...]
    vbuf[y * 4 + z] = vp[...]
    for j in range(1, 16):
        vv(j).start()
    for i in range(NCH):
        cc(i).wait_recv()
        cbuf[i] = cbuf[i] + lg[pl.ds(mine, 32), i * CW:(i + 1) * CW]
        for j in range(1, 16):
            rs(i, j).start()
    for j in range(1, 16):
        vv(j).wait_recv()
    t = vbuf[0]
    for j in range(1, 16):
        t = t + vbuf[j]
    tot[...] = t
    wbuf[ci] = t
    for j in range(1, 8):
        ww(j).start()
    for i in range(NCH):
        a = cbuf[i, pl.ds(pl.multiple_of(y * 8, 8), 8), pl.ds(pl.multiple_of(z * Q, Q), Q)]
        for j in range(1, 16):
            rs(i, j).wait_recv()
            a = a + rbuf[i, j]
        out[pl.ds(pl.multiple_of(mine + y * 8, 8), 8), pl.ds(pl.multiple_of(i * CW + z * Q, Q), Q)] = a * scale_l
        for j in range(1, 16):
            ag(i, j).start()
    a = fp[pl.ds(pl.multiple_of(ci * 8, 8), 8)]
    for j in range(1, 8):
        ff(j).wait_recv()
        a = a + fbuf[j]
    a = a * scale_f
    for t in range(8):
        fo_ref[t] = a[:, t * 128:(t + 1) * 128]
    for i in range(NCH):
        for j in range(1, 16):
            ag(i, j).wait_recv()
        dd(i).start()
    for j in range(1, 8):
        ww(j).wait_recv()
    t = wbuf[0]
    for j in range(1, 8):
        t = t + wbuf[j]
    vo_ref[0, 0] = jnp.sum(t) * scale_v
    outs = []
    for i in range(NCH):
        dd(i).wait_recv()
        c = pltpu.make_async_copy(out.at[:, pl.ds(i * CW, CW)], lo_ref.at[:, pl.ds(i * CW, CW)], lsem.at[i])
        c.start()
        outs.append(c)
    vcopy.wait_send()
    for j in range(1, 16):
        vv(j).wait_send()
    for j in range(1, 8):
        ff(j).wait_send()
        ww(j).wait_send()
    for i in range(NCH):
        cc(i).wait_send()
        dd(i).wait_send()
        for j in range(1, 16):
            rs(i, j).wait_send()
            ag(i, j).wait_send()
    for c in outs:
        c.wait()


def total_sums(lg, fp, v, scale_l, scale_f, scale_v):
    NCH = 2
    CW = 4096 // NCH
    D = pltpu.SemaphoreType.DMA
    vm = pl.BlockSpec(memory_space=V)
    return pl.pallas_call(
        functools.partial(sums, NCH, scale_l, scale_f, scale_v),
        in_specs=[vm, vm, vm],
        out_specs=[pl.BlockSpec(memory_space=pl.ANY), vm, pl.BlockSpec(memory_space=pltpu.SMEM)],
        out_shape=[jax.ShapeDtypeStruct((64, 4096), F32), jax.ShapeDtypeStruct((8, 8, 128), F32), jax.ShapeDtypeStruct((1, 1), F32)],
        scratch_shapes=[V((NCH, 32, CW), F32), V((NCH, 16, 8, CW // 4), F32), V((64, 4096), F32), V((8, 8, 1024), F32),
                        V((8, 128), F32), V((16, 8, 128), F32), V((8, 128), F32), V((8, 8, 128), F32), V((8, 128), F32),
                        D((NCH,)), D((NCH,)), D((NCH, 16)), D((NCH, 16)), D((NCH, 16)), D((NCH, 16)), D((NCH,)), D((NCH,)),
                        D((8,)), D((8,)), D((16,)), D((16,)), D((8,)), D((8,)), D((NCH,))],
        compiler_params=pltpu.CompilerParams(collective_id=0, has_side_effects=True, vmem_limit_bytes=32 << 20),
    )(lg, fp, v)


def per_device(exposures, defaults, base_rate, loadings, factors, weights):
    paths = lax.axis_size("path") * factors.shape[2]
    cptys = lax.axis_size("cpty") * loadings.shape[0]
    lg, fp, v = own_terms(exposures, defaults, base_rate[None, :], loadings.T, factors, weights)
    lo, fo, vo = total_sums(lg, fp, v, 1.0 / paths, factors.shape[1] / cptys, -1.0 / (math.log(2.0) * cptys * paths))
    return vo[0, 0], lo.T, fo


def solution(mesh):
    in_specs = (P("cpty", None, "path"), P("cpty", "path"), P("cpty"), P("cpty", None), P(None, None, "path"), P())
    out_specs = (P(), P("cpty", None), P(None, "cpty", "path"))
    return jax.shard_map(per_device, mesh=mesh, in_specs=in_specs, out_specs=out_specs, check_vma=False)
```

```python
import functools
import math

import jax
import jax.numpy as jnp
from jax import lax
from jax.experimental import pallas as pl
from jax.experimental.pallas import tpu as pltpu
from jax.sharding import PartitionSpec as P

LOG2E = 1.4426950408889634
F32, BF = jnp.float32, jnp.bfloat16
MESH = pl.DeviceIdType.MESH
V = pltpu.VMEM


def split3(v):
    h = v.astype(BF)
    r = v - h.astype(F32)
    m = r.astype(BF)
    return h, m, (r - m.astype(F32)).astype(BF)


CT = 4096
R, RB = 256, 32
NB = CT // R
NDMA = 8
CH = CT // NDMA
CW = 1024
NCH = CT // CW
Q = CW // 4
DEF = 4


def kernel(scale_l, scale_f, scale_v, e_hbm, d_hbm, b_hbm, lt_hbm, f_hbm, w_ref, lo_ref, fo_ref, vo_ref,
           e, d, bv, lt, f, f3, f2, ya, yb, ga, gb, gd, fp, lg, v,
           cbuf, ybuf, ysum, zbuf, rbuf, out, fbuf, vc, vp, vbuf, tot, wbuf,
           dsem, ssem, s_c, r_c, s_y, r_y, s_z, r_z, s_az, r_az, s_ay, r_ay, s_d, r_d, s_r, r_r, s_a, r_a,
           s_f, r_f, s_v, r_v, s_w, r_w):
    ci, pi = lax.axis_index("cpty"), lax.axis_index("path")
    y, z, k = pi // 8, (pi // 2) % 4, pi % 2
    mate = (ci, pi - k + (1 - k))

    def chip(j):
        yy, zz = (y + j // 4) % 4, (z + j % 4) % 4
        return yy, zz, (ci, yy * 8 + zz * 2 + k)

    def fam(j):
        cc_ = (ci + j) % 8
        return cc_, (cc_, pi)

    barrier = pltpu.get_barrier_semaphore()
    for dev in [mate] + [chip(j)[2] for j in range(1, 16)] + [fam(j)[1] for j in range(1, 8)]:
        pl.semaphore_signal(barrier, inc=1, device_id=dev, device_id_type=MESH)

    small = [pltpu.make_async_copy(f_hbm, f, ssem.at[0]), pltpu.make_async_copy(lt_hbm, lt, ssem.at[1]),
             pltpu.make_async_copy(b_hbm, bv, ssem.at[2])]
    for c in small:
        c.start()

    def piece(i):
        s = pl.ds(i * CH, CH)
        return (pltpu.make_async_copy(e_hbm.at[s], e.at[s], dsem.at[0, i]),
                pltpu.make_async_copy(d_hbm.at[s], d.at[s], dsem.at[1, i]))

    for i in range(NDMA):
        for c in piece(i):
            c.start()
    for c in small:
        c.wait()
    f3[...] = jnp.zeros_like(f3)
    for t in range(8):
        h, m, l = split3(f[t].astype(F32) * LOG2E)
        sl = slice(t * 128, (t + 1) * 128)
        f3[0:64, sl] = h
        f3[128:192, sl] = m
        f3[192:256, sl] = l
        f2[:, sl] = f[t]
    row = lax.broadcasted_iota(jnp.int32, (16, 1024), 0)
    f3[64:80, :] = jnp.where(row < 3, 1.0, 0.0).astype(BF)
    fp[...] = jnp.zeros_like(fp)
    v[...] = jnp.zeros_like(v)
    gb[...] = jnp.zeros_like(gb)
    wneg = [-math.log(2.0) * w_ref[t] for t in range(8)]

    def ydot(j, yy):
        cs = pl.ds(pl.multiple_of(j * R, R), R)
        l = lt[:, cs]
        h, m, lo = split3(jnp.log2(bv[:, cs] * (0.5 * LOG2E)))
        row = lax.broadcasted_iota(jnp.int32, (16, R), 0)
        extra = jnp.where(row == 0, h.astype(F32), jnp.where(row == 1, m.astype(F32), jnp.where(row == 2, lo.astype(F32), 0.0))).astype(BF)
        l3 = jnp.concatenate([l, extra, jnp.zeros((48, R), BF), l, l], axis=0)
        yy[...] = lax.dot_general(l3, f3[...], (((0,), (0,)), ((), ())), preferred_element_type=F32)

    def elem(j, yy, gx):
        acc = None
        for q in range(R // RB):
            r = pl.multiple_of(j * R + q * RB, RB)
            rl = slice(q * RB, (q + 1) * RB)
            dd_ = d[pl.ds(r, RB), :]
            es = jnp.swapaxes(e[pl.ds(r, RB)], 0, 1).astype(F32)
            rates, wt, hz = [], [], None
            for t in range(8):
                rt = jnp.exp2(yy[rl, t * 128:(t + 1) * 128])
                hz = -rt if t == 0 else hz - rt
                s = jnp.exp2(hz)
                a = jnp.where(t < dd_, es[t], 0.0) * wneg[t]
                rates.append(rt)
                wt.append(a * s)
            g = None
            for t in range(7, -1, -1):
                g = wt[t] if g is None else g + wt[t]
                gx[rl, t * 128:(t + 1) * 128] = (rates[t] * g).astype(BF)
            for n in range(RB // 8):
                part = g[n * 8:(n + 1) * 8]
                acc = part if acc is None else acc + part
        v[...] += acc

    def ddot(j, gx):
        cs = pl.ds(pl.multiple_of(j * R, R), R)
        lg[:, cs] = lax.dot_general(f2[...], gx[...], (((1,), (1,)), ((), ())), preferred_element_type=F32)

    def edot(j, gx):
        cs = pl.ds(pl.multiple_of(j * R, R), R)
        fp[...] += lax.dot_general(lt[:, cs], gx[...], (((1,), (0,)), ((), ())), preferred_element_type=F32)

    def rc(src, dst, ss, rs_, dev):
        return pltpu.make_async_remote_copy(src, dst, ss, rs_, device_id=dev, device_id_type=MESH)

    mine = pl.multiple_of(k * 32, 32)
    other = pl.multiple_of(32 - k * 32, 32)
    rows = pl.ds(pl.multiple_of(mine + y * 8, 8), 8)

    def ycopy(i, j):
        yy, _, dev = chip(4 * j)
        return rc(cbuf.at[i, pl.ds(pl.multiple_of(yy * 8, 8), 8)], ybuf.at[i, j], s_y.at[i, j], r_y.at[i, j], dev)

    def zcopy(i, j):
        _, zz, dev = chip(j)
        return rc(ysum.at[i, :, pl.ds(pl.multiple_of(zz * Q, Q), Q)], zbuf.at[i, j], s_z.at[i, j], r_z.at[i, j], dev)

    def azcopy(i, j):
        p = out.at[rows, pl.ds(pl.multiple_of(i * CW + z * Q, Q), Q)]
        return rc(p, p, s_az.at[i, j], r_az.at[i, j], chip(j)[2])

    def aycopy(i, j):
        p = out.at[rows, pl.ds(i * CW, CW)]
        return rc(p, p, s_ay.at[i, j], r_ay.at[i, j], chip(4 * j)[2])

    def ccopy(i):
        return rc(lg.at[pl.ds(other, 32), pl.ds(i * CW, CW)], cbuf.at[i], s_c.at[i], r_c.at[i], mate)

    def dcopy(i):
        half = out.at[pl.ds(mine, 32), pl.ds(i * CW, CW)]
        return rc(half, half, s_d.at[i], r_d.at[i], mate)

    def rcopy(j):
        yy, zz, dev = chip(j)
        return rc(cbuf.at[NCH - 1, pl.ds(pl.multiple_of(yy * 8, 8), 8), pl.ds(pl.multiple_of(zz * Q, Q), Q)], rbuf.at[j],
                  s_r.at[j], r_r.at[j], dev)

    def acopy(j):
        p = out.at[rows, pl.ds(pl.multiple_of((NCH - 1) * CW + z * Q, Q), Q)]
        return rc(p, p, s_a.at[j], r_a.at[j], chip(j)[2])

    def fcopy(j):
        cc_, dev = fam(j)
        return rc(fp.at[pl.ds(pl.multiple_of(cc_ * 8, 8), 8)], fbuf.at[j], s_f.at[j], r_f.at[j], dev)

    vcopy = rc(v, vc, s_v.at[0], r_v.at[0], mate)

    def vcopies(j):
        return rc(vp, vbuf.at[y * 4 + z], s_v.at[j], r_v.at[j], chip(j)[2])

    def wcopies(j):
        return rc(tot, wbuf.at[ci], s_w.at[j], r_w.at[j], fam(j)[1])

    def core_out(i):
        ccopy(i).start()

    def core_in(i):
        ccopy(i).wait_recv()
        cbuf[i] = cbuf[i] + lg[pl.ds(mine, 32), i * CW:(i + 1) * CW]

    def y_out(i):
        core_in(i)
        for j in (2, 1, 3):
            ycopy(i, j).start()

    def z_out(i):
        a = cbuf[i, pl.ds(pl.multiple_of(y * 8, 8), 8)]
        for j in range(1, 4):
            ycopy(i, j).wait_recv()
            a = a + ybuf[i, j]
        ysum[i] = a
        for j in range(1, 4):
            zcopy(i, j).start()

    def az_out(i):
        a = ysum[i, :, pl.ds(pl.multiple_of(z * Q, Q), Q)]
        for j in range(1, 4):
            zcopy(i, j).wait_recv()
            a = a + zbuf[i, j]
        out[rows, pl.ds(pl.multiple_of(i * CW + z * Q, Q), Q)] = a * scale_l
        for j in range(1, 4):
            azcopy(i, j).start()

    def ay_out(i):
        for j in range(1, 4):
            azcopy(i, j).wait_recv()
        for j in (2, 1, 3):
            aycopy(i, j).start()

    def d_out(i):
        for j in range(1, 4):
            aycopy(i, j).wait_recv()
        dcopy(i).start()

    steps = [core_out, y_out, z_out, az_out, ay_out, d_out]
    at = {2: [(core_out, 0)], 3: [(y_out, 0)], 4: [(core_out, 1)], 5: [(z_out, 0), (y_out, 1)], 6: [(core_out, 2)],
          7: [(az_out, 0), (z_out, 1), (y_out, 2)]}

    piece_per = CH // (2 * R)
    for c in piece(0):
        c.wait()
    ydot(0, ya)

    def body(n, _):
        if piece_per > 1:
            when = (n % piece_per == 0) & (n > 0)
        else:
            when = n > 0

        @pl.when(when)
        def _():
            for c in piece(n // piece_per):
                c.wait()

        j = 2 * n
        ydot(j + 1, yb)
        elem(j, ya, ga)
        ddot(jnp.maximum(j - 1, 0), gb)
        edot(jnp.maximum(j - 1, 0), gb)

        @pl.when(n == 2)
        def _():
            pl.semaphore_wait(barrier, 23)

        for when_, todo in at.items():
            @pl.when(n == when_)
            def _():
                for step, i in todo:
                    step(i)

        ydot(jnp.minimum(j + 2, NB - 1), ya)
        elem(j + 1, yb, gb)
        ddot(j, ga)
        edot(j, ga)
        return 0

    lax.fori_loop(0, NB // 2, body, 0)
    vcopy.start()
    ddot(NB - 1, gb)
    core_out(3)
    vcopy.wait_recv()
    vp[...] = v[...] + vc[...]
    vbuf[y * 4 + z] = vp[...]
    core_in(3)
    for j in range(15, 0, -1):
        rcopy(j).start()
    for j in range(15, 0, -1):
        vcopies(j).start()
    edot(NB - 1, gb)
    for j in range(7, 0, -1):
        fcopy(j).start()
    ay_out(0)
    az_out(1)
    z_out(2)
    a = cbuf[NCH - 1, pl.ds(pl.multiple_of(y * 8, 8), 8), pl.ds(pl.multiple_of(z * Q, Q), Q)]
    for j in range(1, 16):
        rcopy(j).wait_recv()
        a = a + rbuf[j]
    out[rows, pl.ds(pl.multiple_of((NCH - 1) * CW + z * Q, Q), Q)] = a * scale_l
    for j in range(15, 0, -1):
        acopy(j).start()
    for j in range(1, 16):
        vcopies(j).wait_recv()
    t = vbuf[0]
    for j in range(1, 16):
        t = t + vbuf[j]
    tot[...] = t
    wbuf[ci] = t
    for j in range(7, 0, -1):
        wcopies(j).start()
    d_out(0)
    ay_out(1)
    az_out(2)
    d_out(1)
    ay_out(2)
    a = fp[pl.ds(pl.multiple_of(ci * 8, 8), 8)]
    for j in range(1, 8):
        fcopy(j).wait_recv()
        a = a + fbuf[j]
    a = a * scale_f
    for t in range(8):
        fo_ref[t] = a[:, t * 128:(t + 1) * 128]
    d_out(2)
    for j in range(1, 16):
        acopy(j).wait_recv()
    dcopy(3).start()
    for j in range(1, 8):
        wcopies(j).wait_recv()
    t = wbuf[0]
    for j in range(1, 8):
        t = t + wbuf[j]
    vo_ref[0, 0] = jnp.sum(t) * scale_v
    outs = []
    for i in range(NCH):
        dcopy(i).wait_recv()
        c = pltpu.make_async_copy(out.at[:, pl.ds(i * CW, CW)], lo_ref.at[:, pl.ds(i * CW, CW)], ssem.at[i])
        c.start()
        outs.append(c)
    vcopy.wait_send()
    for j in range(1, 16):
        vcopies(j).wait_send()
        rcopy(j).wait_send()
        acopy(j).wait_send()
    for j in range(1, 8):
        fcopy(j).wait_send()
        wcopies(j).wait_send()
    for i in range(NCH):
        ccopy(i).wait_send()
        dcopy(i).wait_send()
    for i in range(NCH - 1):
        for j in range(1, 4):
            ycopy(i, j).wait_send()
            zcopy(i, j).wait_send()
            azcopy(i, j).wait_send()
            aycopy(i, j).wait_send()
    for c in outs:
        c.wait()


def per_device(exposures, defaults, base_rate, loadings, factors, weights):
    paths = lax.axis_size("path") * factors.shape[2]
    cptys = lax.axis_size("cpty") * loadings.shape[0]
    scales = 1.0 / paths, factors.shape[1] / cptys, -1.0 / (math.log(2.0) * cptys * paths)
    A = pl.BlockSpec(memory_space=pl.ANY)
    D = pltpu.SemaphoreType.DMA
    lo, fo, vo = pl.pallas_call(
        functools.partial(kernel, *scales),
        in_specs=[A, A, A, A, A, pl.BlockSpec(memory_space=pltpu.SMEM)],
        out_specs=[A, pl.BlockSpec(memory_space=V), pl.BlockSpec(memory_space=pltpu.SMEM)],
        out_shape=[jax.ShapeDtypeStruct((64, CT), F32), jax.ShapeDtypeStruct((8, 8, 128), F32), jax.ShapeDtypeStruct((1, 1), F32)],
        scratch_shapes=[
            V((CT, 8, 128), BF), V((CT, 128), jnp.int32), V((1, CT), F32), V((64, CT), BF), V((8, 64, 128), BF),
            V((256, 1024), BF), V((64, 1024), BF), V((R, 1024), F32), V((R, 1024), F32), V((R, 1024), BF), V((R, 1024), BF), V((R, 1024), BF),
            V((64, 1024), F32), V((64, CT), F32), V((8, 128), F32),
            V((NCH, 32, CW), F32), V((NCH, 4, 8, CW), F32), V((NCH, 8, CW), F32), V((NCH, 4, 8, Q), F32), V((16, 8, Q), F32), V((64, CT), F32),
            V((8, 8, 1024), F32), V((8, 128), F32), V((8, 128), F32), V((16, 8, 128), F32), V((8, 128), F32), V((8, 8, 128), F32),
            D((2, NDMA)), D((4,)), D((NCH,)), D((NCH,)), D((NCH, 4)), D((NCH, 4)), D((NCH, 4)), D((NCH, 4)), D((NCH, 4)), D((NCH, 4)),
            D((NCH, 4)), D((NCH, 4)), D((NCH,)), D((NCH,)), D((16,)), D((16,)), D((16,)), D((16,)),
            D((8,)), D((8,)), D((16,)), D((16,)), D((8,)), D((8,))],
        compiler_params=pltpu.CompilerParams(collective_id=0, has_side_effects=True, vmem_limit_bytes=60 << 20),
        name="adjoint",
    )(exposures, defaults, base_rate[None, :], loadings.T, factors, weights)
    return vo[0, 0], lo.T, fo


def solution(mesh):
    in_specs = (P("cpty", None, "path"), P("cpty", "path"), P("cpty"), P("cpty", None), P(None, None, "path"), P())
    out_specs = (P(), P("cpty", None), P(None, "cpty", "path"))
    return jax.shard_map(per_device, mesh=mesh, in_specs=in_specs, out_specs=out_specs, check_vma=False)
```

```python
import functools
import math

import jax
import jax.numpy as jnp
from jax import lax
from jax.experimental import pallas as pl
from jax.experimental.pallas import tpu as pltpu
from jax.sharding import PartitionSpec as P

LOG2E = 1.4426950408889634
F32, BF = jnp.float32, jnp.bfloat16
MESH = pl.DeviceIdType.MESH
V = pltpu.VMEM


def split3(v):
    h = v.astype(BF)
    r = v - h.astype(F32)
    m = r.astype(BF)
    return h, m, (r - m.astype(F32)).astype(BF)


CT = 4096
R, RB = 256, 16
NB = CT // R
CH = 2 * R
AHEAD = 4
ENDS = (1280, 2304, 3328, 4096)


def kernel(scale_l, scale_f, scale_v, e_hbm, d_hbm, b_hbm, lt_hbm, f_hbm, w_ref, lo_ref, fo_ref, vo_ref,
           e, d, bv, lt, f, f3, f2, ya, yb, et, gall, fp, lg, v, cbuf, ybuf, zbuf, fx, fz, vc, vy, vx, vz,
           dsem, ssem, s_c, r_c, s_y, r_y, s_z, r_z, s_a, r_a, s_d, r_d, s_f, r_f, s_v, r_v):
    ci, pi = lax.axis_index("cpty"), lax.axis_index("path")
    zh, x = ci // 4, ci % 4
    y, z, k = pi // 8, (pi // 2) % 4, pi % 2
    z8 = zh * 4 + z
    mate = (ci, pi - k + (1 - k))

    def ypeer(j):
        yy = (y + j) % 4
        return yy, (ci, yy * 8 + z * 2 + k)

    def zpeer(j):
        return (ci, y * 8 + ((z + j) % 4) * 2 + k)

    def xpeer(j):
        xx = (x + j) % 4
        return xx, (zh * 4 + xx, pi)

    def ringpeer(j):
        zz = (z8 + j) % 8
        return ((zz // 4) * 4 + x, y * 8 + (zz % 4) * 2 + k)

    zhpeer = ((1 - zh) * 4 + x, pi)

    small = [pltpu.make_async_copy(f_hbm, f, ssem.at[0]), pltpu.make_async_copy(lt_hbm, lt, ssem.at[1]),
             pltpu.make_async_copy(b_hbm, bv, ssem.at[2])]
    for c in small:
        c.start()

    def piece(i):
        s = pl.ds(pl.multiple_of(i * CH, CH), CH)
        return (pltpu.make_async_copy(e_hbm.at[s], e.at[s], dsem.at[0, i]),
                pltpu.make_async_copy(d_hbm.at[s], d.at[s], dsem.at[1, i]))

    for i in range(AHEAD):
        for c in piece(i):
            c.start()
    barrier = pltpu.get_barrier_semaphore()
    peers = [mate] + [ypeer(j)[1] for j in range(1, 4)] + [xpeer(j)[1] for j in range(1, 4)] + [ringpeer(j) for j in range(1, 8)]
    for dev in peers:
        pl.semaphore_signal(barrier, inc=1, device_id=dev, device_id_type=MESH)
    f3[64:128, :] = jnp.zeros((64, 1024), BF)
    row = lax.broadcasted_iota(jnp.int32, (16, 1024), 0)
    f3[64:80, :] = jnp.where(row < 3, 1.0, 0.0).astype(BF)
    v[...] = jnp.zeros_like(v)
    gall[pl.ds(0, R), :] = jnp.zeros((R, 1024), BF)
    for c in small:
        c.wait()
    for t in range(8):
        h, m, l = split3(f[t].astype(F32) * LOG2E)
        sl = slice(t * 128, (t + 1) * 128)
        f3[0:64, sl] = h
        f3[128:192, sl] = m
        f3[192:256, sl] = l
        f2[:, sl] = f[t]
    wneg = [-math.log(2.0) * w_ref[t] for t in range(8)]

    def ydot(j, yy):
        cs = pl.ds(pl.multiple_of(j * R, R), R)
        l = lt[:, cs]
        h, m, lo = split3(jnp.log2(bv[:, cs] * (0.5 * LOG2E)))
        row = lax.broadcasted_iota(jnp.int32, (16, R), 0)
        extra = jnp.where(row == 0, h.astype(F32), jnp.where(row == 1, m.astype(F32), jnp.where(row == 2, lo.astype(F32), 0.0))).astype(BF)
        l3 = jnp.concatenate([l, extra, jnp.zeros((48, R), BF), l, l], axis=0)
        yy[...] = lax.dot_general(l3, f3[...], (((0,), (0,)), ((), ())), preferred_element_type=F32)

    def elem(j, yy):
        acc = None
        for q in range(R // RB):
            r = pl.multiple_of(j * R + q * RB, RB)
            rl = slice(q * RB, (q + 1) * RB)
            dd_ = d[pl.ds(r, RB), :]
            et[q * RB * 8:(q + 1) * RB * 8, :] = e[pl.ds(r, RB)].astype(F32).reshape(RB * 8, 128)
            rates, wt, hz = [], [], None
            for t in range(8):
                rt = jnp.exp2(yy[rl, t * 128:(t + 1) * 128])
                hz = -rt if t == 0 else hz - rt
                s = jnp.exp2(hz)
                a = jnp.where(t < dd_, et[pl.ds(q * RB * 8 + t, RB, stride=8), :], 0.0) * wneg[t]
                rates.append(rt)
                wt.append(a * s)
            g = None
            for t in range(7, -1, -1):
                g = wt[t] if g is None else g + wt[t]
                gall[pl.ds(r, RB), t * 128:(t + 1) * 128] = (rates[t] * g).astype(BF)
            for n in range(RB // 8):
                part = g[n * 8:(n + 1) * 8]
                acc = part if acc is None else acc + part
        v[...] += acc

    def ddot(j):
        cs = pl.ds(pl.multiple_of(j * R, R), R)
        lg[:, cs] = lax.dot_general(f2[...], gall[cs, :], (((1,), (1,)), ((), ())), preferred_element_type=F32)

    def rc(src, dst, ss, rs_, dev):
        return pltpu.make_async_remote_copy(src, dst, ss, rs_, device_id=dev, device_id_type=MESH)

    mine = pl.multiple_of(k * 32, 32)
    other = pl.multiple_of(32 - k * 32, 32)
    rows = pl.ds(pl.multiple_of(mine + y * 8, 8), 8)

    def cols(i):
        lo = 0 if i == 0 else ENDS[i - 1]
        return pl.ds(lo, ENDS[i] - lo)

    def ccopy(i):
        return rc(lg.at[pl.ds(other, 32), cols(i)], cbuf.at[:, cols(i)], s_c.at[i], r_c.at[i], mate)

    def ycopy(i, j):
        yy, dev = ypeer(j)
        return rc(cbuf.at[pl.ds(pl.multiple_of(yy * 8, 8), 8), cols(i)], ybuf.at[j, :, cols(i)], s_y.at[i, j], r_y.at[i, j], dev)

    def zcopy(i, j):
        p = zbuf.at[z, :, cols(i)]
        return rc(p, p, s_z.at[i, j], r_z.at[i, j], zpeer(j))

    def acopy(i, j):
        p = lo_ref.at[rows, cols(i)]
        return rc(p, p, s_a.at[i, j], r_a.at[i, j], ypeer(j)[1])

    def dcopy(i):
        half = lo_ref.at[pl.ds(mine, 32), cols(i)]
        return rc(half, half, s_d.at[i], r_d.at[i], mate)

    def core_out(i):
        ccopy(i).start()

    def y_out(i):
        ccopy(i).wait_recv()
        cbuf[:, cols(i)] = cbuf[:, cols(i)] + lg[pl.ds(mine, 32), cols(i)]
        for j in (2, 1, 3):
            ycopy(i, j).start()

    def z_out(i):
        a = cbuf[pl.ds(pl.multiple_of(y * 8, 8), 8), cols(i)]
        for j in range(1, 4):
            ycopy(i, j).wait_recv()
            a = a + ybuf[j, :, cols(i)]
        zbuf[z, :, cols(i)] = a
        for j in range(1, 4):
            zcopy(i, j).start()

    def a_out(i):
        for j in range(1, 4):
            zcopy(i, j).wait_recv()
        a = (zbuf[0, :, cols(i)] + zbuf[1, :, cols(i)]) + (zbuf[2, :, cols(i)] + zbuf[3, :, cols(i)])
        lo_ref[rows, cols(i)] = a * scale_l
        for j in (2, 1, 3):
            acopy(i, j).start()

    def d_out(i):
        for j in range(1, 4):
            acopy(i, j).wait_recv()
        dcopy(i).start()

    def fcopy(j):
        xx, dev = xpeer(j)
        return rc(fp.at[:, xx], fx.at[j], s_f.at[j], r_f.at[j], dev)

    fzcopy = rc(fz.at[1 - zh], fz.at[2], s_f.at[0], r_f.at[0], zhpeer)
    vcopy = rc(v, vc, s_v.at[0], r_v.at[0], mate)

    def vycopy(j):
        return rc(vy.at[y], vy.at[y], s_v.at[j], r_v.at[j], ypeer(j)[1])

    def vxcopy(j):
        return rc(vx.at[x], vx.at[x], s_v.at[3 + j], r_v.at[3 + j], xpeer(j)[1])

    def vzcopy(j):
        return rc(vz.at[z8], vz.at[z8], s_v.at[6 + j], r_v.at[6 + j], ringpeer(j))

    at = {2: [(core_out, 0)], 3: [(y_out, 0)], 4: [(core_out, 1)], 5: [(y_out, 1)], 6: [(core_out, 2), (z_out, 0)], 7: [(y_out, 2)]}

    ydot(0, ya)

    def body(n, _):
        @pl.when(n < NB // 2 - AHEAD)
        def _():
            for c in piece(n + AHEAD):
                c.start()

        for c in piece(n):
            c.wait()
        j = 2 * n
        ydot(j + 1, yb)
        elem(j, ya)
        ddot(jnp.maximum(j - 1, 0))
        ydot(jnp.minimum(j + 2, NB - 1), ya)
        elem(j + 1, yb)
        ddot(j)

        @pl.when(n == 2)
        def _():
            pl.semaphore_wait(barrier, len(peers))

        for when_, todo in at.items():
            @pl.when(n == when_)
            def _():
                for step, i in todo:
                    step(i)

        return 0

    lax.fori_loop(0, NB // 2, body, 0)
    ddot(NB - 1)
    core_out(3)
    vcopy.start()
    z_out(1)
    y_out(3)
    vcopy.wait_recv()
    vy[y] = v[...] + vc[...]
    for j in (2, 1, 3):
        vycopy(j).start()
    for t in range(0, 8, 2):
        part = lax.dot_general(lt[...], gall[:, t * 128:(t + 2) * 128], (((1,), (0,)), ((), ())), preferred_element_type=F32)
        fp[:, :, :, t * 128:(t + 2) * 128] = part.reshape(2, 4, 8, 256)
    for j in (2, 1, 3):
        fcopy(j).start()
    z_out(2)
    for j in range(1, 4):
        vycopy(j).wait_recv()
    vx[x] = (vy[0] + vy[1]) + (vy[2] + vy[3])
    for j in (2, 1, 3):
        vxcopy(j).start()
    z_out(3)
    a_out(0)
    a_out(1)
    for j in range(1, 4):
        vxcopy(j).wait_recv()
    vz[z8] = (vx[0] + vx[1]) + (vx[2] + vx[3])
    for j in (4, 3, 5, 2, 6, 1, 7):
        vzcopy(j).start()
    a = fp[:, x]
    for j in range(1, 4):
        fcopy(j).wait_recv()
        a = a + fx[j]
    fz[0:2] = a
    fzcopy.start()
    a_out(2)
    d_out(0)
    a_out(3)
    d_out(1)
    for j in range(1, 8):
        vzcopy(j).wait_recv()
    a = ((vz[0] + vz[1]) + (vz[2] + vz[3])) + ((vz[4] + vz[5]) + (vz[6] + vz[7]))
    vo_ref[0, 0] = jnp.sum(a) * scale_v
    fzcopy.wait_recv()
    a = (fz[zh] + fz[2]) * scale_f
    for t in range(8):
        fo_ref[t] = a[:, t * 128:(t + 1) * 128]
    d_out(2)
    d_out(3)
    vcopy.wait_send()
    fzcopy.wait_send()
    for j in range(1, 4):
        vycopy(j).wait_send()
        vxcopy(j).wait_send()
        fcopy(j).wait_send()
    for j in range(1, 8):
        vzcopy(j).wait_send()
    for i in range(4):
        ccopy(i).wait_send()
        for j in range(1, 4):
            ycopy(i, j).wait_send()
            zcopy(i, j).wait_send()
            acopy(i, j).wait_send()
        dcopy(i).wait_recv()
        dcopy(i).wait_send()


def per_device(exposures, defaults, base_rate, loadings, factors, weights):
    paths = lax.axis_size("path") * factors.shape[2]
    cptys = lax.axis_size("cpty") * loadings.shape[0]
    scales = 1.0 / paths, factors.shape[1] / cptys, -1.0 / (math.log(2.0) * cptys * paths)
    A = pl.BlockSpec(memory_space=pl.ANY)
    H = pl.BlockSpec(memory_space=pltpu.HBM)
    S = pl.BlockSpec(memory_space=pltpu.SMEM)
    D = pltpu.SemaphoreType.DMA
    shapes = [jax.ShapeDtypeStruct((64, CT), F32), jax.ShapeDtypeStruct((8, 8, 128), F32), jax.ShapeDtypeStruct((1, 1), F32)]
    lo, fo, vo = pl.pallas_call(
        functools.partial(kernel, *scales),
        in_specs=[H, H, H, H, H, S],
        out_specs=[pl.BlockSpec(memory_space=V), pl.BlockSpec(memory_space=V), S],
        out_shape=shapes,
        scratch_shapes=[
            V((CT, 8, 128), BF), V((CT, 128), jnp.int32), V((1, CT), F32), V((64, CT), BF), V((8, 64, 128), BF),
            V((256, 1024), BF), V((64, 1024), BF), V((R, 1024), F32), V((R, 1024), F32), V((R * 8, 128), F32), V((CT, 1024), BF),
            V((2, 4, 8, 1024), F32), V((64, CT), F32), V((8, 128), F32),
            V((32, CT), F32), V((4, 8, CT), F32), V((4, 8, CT), F32),
            V((4, 2, 8, 1024), F32), V((3, 8, 1024), F32), V((8, 128), F32), V((4, 8, 128), F32), V((4, 8, 128), F32), V((8, 8, 128), F32),
            D((2, NB // 2)), D((4,)), D((4,)), D((4,)), D((4, 4)), D((4, 4)), D((4, 4)), D((4, 4)), D((4, 4)), D((4, 4)), D((4,)), D((4,)),
            D((4,)), D((4,)), D((16,)), D((16,))],
        compiler_params=pltpu.CompilerParams(collective_id=0, has_side_effects=True, vmem_limit_bytes=44 << 20),
        name="adjoint",
    )(*(pltpu.with_memory_space_constraint(a, pltpu.HBM) for a in (exposures, defaults, base_rate[None, :], loadings.T, factors, weights)))
    return vo[0, 0], lo.T, fo


def solution(mesh):
    in_specs = (P("cpty", None, "path"), P("cpty", "path"), P("cpty"), P("cpty", None), P(None, None, "path"), P())
    out_specs = (P(), P("cpty", None), P(None, "cpty", "path"))
    return jax.shard_map(per_device, mesh=mesh, in_specs=in_specs, out_specs=out_specs, check_vma=False)
```

```python
import functools
import math

import jax
import jax.numpy as jnp
from jax import lax
from jax.experimental import pallas as pl
from jax.experimental.pallas import tpu as pltpu
from jax.sharding import PartitionSpec as P

LOG2E = 1.4426950408889634
F32, BF = jnp.float32, jnp.bfloat16
MESH = pl.DeviceIdType.MESH
V = pltpu.VMEM


def split3(v):
    h = v.astype(BF)
    r = v - h.astype(F32)
    m = r.astype(BF)
    return h, m, (r - m.astype(F32)).astype(BF)


CT = 4096
R, RB = 256, 16
NB = CT // R
CH = 2 * R
AHEAD = 1
ENDS = (1280, 2304, 3328, 4096)


def kernel(scale_l, scale_f, scale_v, e_hbm, d_hbm, b_hbm, lt_hbm, f_hbm, w_ref, lo_ref, fo_ref, vo_ref,
           e, d, bv, lt, f, f3, f2, ya, yb, et, gall, fp, lg, v, cbuf, ybuf, zbuf, fx, fz, vc, vy, vx, vz,
           dsem, ssem, s_c, r_c, s_y, r_y, s_z, r_z, s_a, r_a, s_d, r_d, s_f, r_f, s_v, r_v):
    ci, pi = lax.axis_index("cpty"), lax.axis_index("path")
    zh, x = ci // 4, ci % 4
    y, z, k = pi // 8, (pi // 2) % 4, pi % 2
    z8 = zh * 4 + z
    mate = (ci, pi - k + (1 - k))

    def ypeer(j):
        yy = (y + j) % 4
        return yy, (ci, yy * 8 + z * 2 + k)

    def zpeer(j):
        return (ci, y * 8 + ((z + j) % 4) * 2 + k)

    def xpeer(j):
        xx = (x + j) % 4
        return xx, (zh * 4 + xx, pi)

    def ringpeer(j):
        zz = (z8 + j) % 8
        return ((zz // 4) * 4 + x, y * 8 + (zz % 4) * 2 + k)

    zhpeer = ((1 - zh) * 4 + x, pi)

    small = [pltpu.make_async_copy(f_hbm, f, ssem.at[0]), pltpu.make_async_copy(lt_hbm, lt, ssem.at[1]),
             pltpu.make_async_copy(b_hbm, bv, ssem.at[2])]
    for c in small:
        c.start()

    def piece(i):
        s = pl.ds(pl.multiple_of(i * CH, CH), CH)
        return (pltpu.make_async_copy(e_hbm.at[s], e.at[s], dsem.at[0, i]),
                pltpu.make_async_copy(d_hbm.at[s], d.at[s], dsem.at[1, i]))

    for i in range(AHEAD):
        for c in piece(i):
            c.start()
    barrier = pltpu.get_barrier_semaphore()
    peers = [mate] + [ypeer(j)[1] for j in range(1, 4)] + [xpeer(j)[1] for j in range(1, 4)] + [ringpeer(j) for j in range(1, 8)]
    for dev in peers:
        pl.semaphore_signal(barrier, inc=1, device_id=dev, device_id_type=MESH)
    f3[64:128, :] = jnp.zeros((64, 1024), BF)
    row = lax.broadcasted_iota(jnp.int32, (16, 1024), 0)
    f3[64:80, :] = jnp.where(row < 3, 1.0, 0.0).astype(BF)
    v[...] = jnp.zeros_like(v)
    gall[pl.ds(0, R), :] = jnp.zeros((R, 1024), BF)
    for c in small:
        c.wait()
    for t in range(8):
        h, m, l = split3(f[t].astype(F32) * LOG2E)
        sl = slice(t * 128, (t + 1) * 128)
        f3[0:64, sl] = h
        f3[128:192, sl] = m
        f3[192:256, sl] = l
        f2[:, sl] = f[t]
    wneg = [-math.log(2.0) * w_ref[t] for t in range(8)]

    def ydot(j, yy):
        cs = pl.ds(pl.multiple_of(j * R, R), R)
        l = lt[:, cs]
        h, m, lo = split3(jnp.log2(bv[:, cs] * (0.5 * LOG2E)))
        row = lax.broadcasted_iota(jnp.int32, (16, R), 0)
        extra = jnp.where(row == 0, h.astype(F32), jnp.where(row == 1, m.astype(F32), jnp.where(row == 2, lo.astype(F32), 0.0))).astype(BF)
        l3 = jnp.concatenate([l, extra, jnp.zeros((48, R), BF), l, l], axis=0)
        yy[...] = lax.dot_general(l3, f3[...], (((0,), (0,)), ((), ())), preferred_element_type=F32)

    def elem(j, yy):
        acc = None
        for q in range(R // RB):
            r = pl.multiple_of(j * R + q * RB, RB)
            rl = slice(q * RB, (q + 1) * RB)
            dd_ = d[pl.ds(r, RB), :]
            et[q * RB * 8:(q + 1) * RB * 8, :] = e[pl.ds(r, RB)].astype(F32).reshape(RB * 8, 128)
            sums = []
            for o in range(0, RB, 8):
                rates, wt, hz = [], [], None
                for t in range(8):
                    rt = jnp.exp2(yy[q * RB + o:q * RB + o + 8, t * 128:(t + 1) * 128])
                    hz = -rt if t == 0 else hz - rt
                    s = jnp.exp2(hz)
                    a = jnp.where(t < dd_[o:o + 8], et[pl.ds((q * RB + o) * 8 + t, 8, stride=8), :], 0.0) * wneg[t]
                    rates.append(rt)
                    wt.append(a * s)
                g = None
                for t in range(7, -1, -1):
                    g = wt[t] if g is None else g + wt[t]
                    rates[t] = rates[t] * g
                sums.append(rates)
                acc = g if acc is None else acc + g
            for t in range(8):
                gall[pl.ds(r, RB), t * 128:(t + 1) * 128] = jnp.concatenate([rates[t] for rates in sums], axis=0).astype(BF)
        v[...] += acc

    def ddot(j):
        cs = pl.ds(pl.multiple_of(j * R, R), R)
        lg[:, cs] = lax.dot_general(f2[...], gall[cs, :], (((1,), (1,)), ((), ())), preferred_element_type=F32)

    def rc(src, dst, ss, rs_, dev):
        return pltpu.make_async_remote_copy(src, dst, ss, rs_, device_id=dev, device_id_type=MESH)

    mine = pl.multiple_of(k * 32, 32)
    other = pl.multiple_of(32 - k * 32, 32)
    rows = pl.ds(pl.multiple_of(mine + y * 8, 8), 8)

    def cols(i):
        lo = 0 if i == 0 else ENDS[i - 1]
        return pl.ds(lo, ENDS[i] - lo)

    def ccopy(i):
        return rc(lg.at[pl.ds(other, 32), cols(i)], cbuf.at[:, cols(i)], s_c.at[i], r_c.at[i], mate)

    def ycopy(i, j):
        yy, dev = ypeer(j)
        return rc(cbuf.at[pl.ds(pl.multiple_of(yy * 8, 8), 8), cols(i)], ybuf.at[j, :, cols(i)], s_y.at[i, j], r_y.at[i, j], dev)

    def zcopy(i, j):
        p = zbuf.at[z, :, cols(i)]
        return rc(p, p, s_z.at[i, j], r_z.at[i, j], zpeer(j))

    def acopy(i, j):
        p = lo_ref.at[rows, cols(i)]
        return rc(p, p, s_a.at[i, j], r_a.at[i, j], ypeer(j)[1])

    def dcopy(i):
        half = lo_ref.at[pl.ds(mine, 32), cols(i)]
        return rc(half, half, s_d.at[i], r_d.at[i], mate)

    def core_out(i):
        ccopy(i).start()

    def y_out(i):
        ccopy(i).wait_recv()
        cbuf[:, cols(i)] = cbuf[:, cols(i)] + lg[pl.ds(mine, 32), cols(i)]
        for j in (2, 1, 3):
            ycopy(i, j).start()

    def z_out(i):
        a = cbuf[pl.ds(pl.multiple_of(y * 8, 8), 8), cols(i)]
        for j in range(1, 4):
            ycopy(i, j).wait_recv()
            a = a + ybuf[j, :, cols(i)]
        zbuf[z, :, cols(i)] = a
        for j in range(1, 4):
            zcopy(i, j).start()

    def a_out(i):
        for j in range(1, 4):
            zcopy(i, j).wait_recv()
        a = (zbuf[0, :, cols(i)] + zbuf[1, :, cols(i)]) + (zbuf[2, :, cols(i)] + zbuf[3, :, cols(i)])
        lo_ref[rows, cols(i)] = a * scale_l
        for j in (2, 1, 3):
            acopy(i, j).start()

    def d_out(i):
        for j in range(1, 4):
            acopy(i, j).wait_recv()
        dcopy(i).start()

    def fcopy(j):
        xx, dev = xpeer(j)
        return rc(fp.at[:, xx], fx.at[j], s_f.at[j], r_f.at[j], dev)

    fzcopy = rc(fz.at[1 - zh], fz.at[2], s_f.at[0], r_f.at[0], zhpeer)
    vcopy = rc(v, vc, s_v.at[0], r_v.at[0], mate)

    def vycopy(j):
        return rc(vy.at[y], vy.at[y], s_v.at[j], r_v.at[j], ypeer(j)[1])

    def vxcopy(j):
        return rc(vx.at[x], vx.at[x], s_v.at[3 + j], r_v.at[3 + j], xpeer(j)[1])

    def vzcopy(j):
        return rc(vz.at[z8], vz.at[z8], s_v.at[6 + j], r_v.at[6 + j], ringpeer(j))

    at = {2: [(core_out, 0)], 3: [(y_out, 0)], 4: [(core_out, 1)], 5: [(y_out, 1)], 6: [(core_out, 2), (z_out, 0)], 7: [(y_out, 2)]}

    ydot(0, ya)

    def body(n, _):
        @pl.when(n < NB // 2 - AHEAD)
        def _():
            for c in piece(n + AHEAD):
                c.start()

        for c in piece(n):
            c.wait()
        j = 2 * n
        ydot(j + 1, yb)
        elem(j, ya)
        ddot(jnp.maximum(j - 1, 0))
        ydot(jnp.minimum(j + 2, NB - 1), ya)
        elem(j + 1, yb)
        ddot(j)

        @pl.when(n == 2)
        def _():
            pl.semaphore_wait(barrier, len(peers))

        for when_, todo in at.items():
            @pl.when(n == when_)
            def _():
                for step, i in todo:
                    step(i)

        return 0

    lax.fori_loop(0, NB // 2, body, 0)
    ddot(NB - 1)
    core_out(3)
    vcopy.start()
    z_out(1)
    y_out(3)
    vcopy.wait_recv()
    vy[y] = v[...] + vc[...]
    for j in (2, 1, 3):
        vycopy(j).start()
    for t in range(0, 8, 2):
        part = lax.dot_general(lt[...], gall[:, t * 128:(t + 2) * 128], (((1,), (0,)), ((), ())), preferred_element_type=F32)
        fp[:, :, :, t * 128:(t + 2) * 128] = part.reshape(2, 4, 8, 256)
    for j in (2, 1, 3):
        fcopy(j).start()
    z_out(2)
    for j in range(1, 4):
        vycopy(j).wait_recv()
    vx[x] = (vy[0] + vy[1]) + (vy[2] + vy[3])
    for j in (2, 1, 3):
        vxcopy(j).start()
    z_out(3)
    a_out(0)
    a_out(1)
    for j in range(1, 4):
        vxcopy(j).wait_recv()
    vz[z8] = (vx[0] + vx[1]) + (vx[2] + vx[3])
    for j in (4, 3, 5, 2, 6, 1, 7):
        vzcopy(j).start()
    a = fp[:, x]
    for j in range(1, 4):
        fcopy(j).wait_recv()
        a = a + fx[j]
    fz[0:2] = a
    fzcopy.start()
    a_out(2)
    d_out(0)
    a_out(3)
    d_out(1)
    for j in range(1, 8):
        vzcopy(j).wait_recv()
    a = ((vz[0] + vz[1]) + (vz[2] + vz[3])) + ((vz[4] + vz[5]) + (vz[6] + vz[7]))
    vo_ref[...] = jnp.sum(a, axis=(0, 1), keepdims=True) * scale_v
    fzcopy.wait_recv()
    a = (fz[zh] + fz[2]) * scale_f
    for t in range(8):
        fo_ref[t] = a[:, t * 128:(t + 1) * 128]
    d_out(2)
    d_out(3)
    vcopy.wait_send()
    fzcopy.wait_send()
    for j in range(1, 4):
        vycopy(j).wait_send()
        vxcopy(j).wait_send()
        fcopy(j).wait_send()
    for j in range(1, 8):
        vzcopy(j).wait_send()
    for i in range(4):
        ccopy(i).wait_send()
        for j in range(1, 4):
            ycopy(i, j).wait_send()
            zcopy(i, j).wait_send()
            acopy(i, j).wait_send()
        dcopy(i).wait_recv()
        dcopy(i).wait_send()


def finish(lo, fo, vo, lo_ref, fo_ref, vo_ref, sem):
    copies = [pltpu.make_async_copy(lo.at[pl.ds(8 * i, 8)], lo_ref.at[pl.ds(8 * i, 8)], sem.at[i]) for i in range(8)]
    copies += [pltpu.make_async_copy(fo, fo_ref, sem.at[8]), pltpu.make_async_copy(vo, vo_ref, sem.at[9])]
    for c in copies:
        c.start()
    for c in copies:
        c.wait()


def per_device(exposures, defaults, base_rate, loadings, factors, weights):
    paths = lax.axis_size("path") * factors.shape[2]
    cptys = lax.axis_size("cpty") * loadings.shape[0]
    scales = 1.0 / paths, factors.shape[1] / cptys, -1.0 / (math.log(2.0) * cptys * paths)
    A = pl.BlockSpec(memory_space=pl.ANY)
    H = pl.BlockSpec(memory_space=pltpu.HBM)
    S = pl.BlockSpec(memory_space=pltpu.SMEM)
    D = pltpu.SemaphoreType.DMA
    shapes = [jax.ShapeDtypeStruct((64, CT), F32), jax.ShapeDtypeStruct((8, 8, 128), F32), jax.ShapeDtypeStruct((1, 1), F32)]
    lo, fo, vo = pl.pallas_call(
        functools.partial(kernel, *scales),
        in_specs=[H, H, H, H, H, S],
        out_specs=[pl.BlockSpec(memory_space=V)] * 3,
        out_shape=shapes,
        scratch_shapes=[
            V((CT, 8, 128), BF), V((CT, 128), jnp.int32), V((1, CT), F32), V((64, CT), BF), V((8, 64, 128), BF),
            V((256, 1024), BF), V((64, 1024), BF), V((R, 1024), F32), V((R, 1024), F32), V((R * 8, 128), F32), V((CT, 1024), BF),
            V((2, 4, 8, 1024), F32), V((64, CT), F32), V((8, 128), F32),
            V((32, CT), F32), V((4, 8, CT), F32), V((4, 8, CT), F32),
            V((4, 2, 8, 1024), F32), V((3, 8, 1024), F32), V((8, 128), F32), V((4, 8, 128), F32), V((4, 8, 128), F32), V((8, 8, 128), F32),
            D((2, NB // 2)), D((4,)), D((4,)), D((4,)), D((4, 4)), D((4, 4)), D((4, 4)), D((4, 4)), D((4, 4)), D((4, 4)), D((4,)), D((4,)),
            D((4,)), D((4,)), D((16,)), D((16,))],
        compiler_params=pltpu.CompilerParams(collective_id=0, has_side_effects=True, vmem_limit_bytes=44 << 20),
        name="adjoint",
    )(*(pltpu.with_memory_space_constraint(a, pltpu.HBM) for a in (exposures, defaults, base_rate[None, :], loadings.T, factors, weights)))
    lo, fo, vo = (pltpu.with_memory_space_constraint(a, pltpu.VMEM) for a in (lo, fo, vo))
    lo, fo, vo = pl.pallas_call(
        finish,
        in_specs=[A, A, A],
        out_specs=[H, H, H],
        out_shape=shapes,
        scratch_shapes=[D((10,))],
        name="finish",
    )(lo, fo, vo)
    return vo[0, 0], lo.T, fo


def solution(mesh):
    in_specs = (P("cpty", None, "path"), P("cpty", "path"), P("cpty"), P("cpty", None), P(None, None, "path"), P())
    out_specs = (P(), P("cpty", None), P(None, "cpty", "path"))
    return jax.shard_map(per_device, mesh=mesh, in_specs=in_specs, out_specs=out_specs, check_vma=False)
```

```python
import functools
import math

import jax
import jax.numpy as jnp
from jax import lax
from jax.experimental import pallas as pl
from jax.experimental.pallas import tpu as pltpu
from jax.sharding import PartitionSpec as P

LOG2E = 1.4426950408889634
F32, BF = jnp.float32, jnp.bfloat16
MESH = pl.DeviceIdType.MESH
V = pltpu.VMEM


def split3(v):
    h = v.astype(BF)
    r = v - h.astype(F32)
    m = r.astype(BF)
    return h, m, (r - m.astype(F32)).astype(BF)


CT = 4096
R, RB = 256, 16
NB = CT // R
CH = 2 * R
AHEAD = 1
ENDS = (1280, 2304, 3328, 4096)


def kernel(scale_l, scale_f, scale_v, e_hbm, d_hbm, b_hbm, lt_hbm, f_hbm, w_hbm, lo_ref, fo_ref, vo_ref,
           e, d, bv, lt, f, f3, f2, ya, yb, et, gall, fp, lg, v, cbuf, ybuf, zbuf, fx, fz, vc, vy, vx, vz,
           w_ref, dsem, ssem, s_c, r_c, s_y, r_y, s_z, r_z, s_a, r_a, s_d, r_d, s_f, r_f, s_v, r_v):
    ci, pi = lax.axis_index("cpty"), lax.axis_index("path")
    zh, x = ci // 4, ci % 4
    y, z, k = pi // 8, (pi // 2) % 4, pi % 2
    z8 = zh * 4 + z
    mate = (ci, pi - k + (1 - k))

    def ypeer(j):
        yy = (y + j) % 4
        return yy, (ci, yy * 8 + z * 2 + k)

    def zpeer(j):
        return (ci, y * 8 + ((z + j) % 4) * 2 + k)

    def xpeer(j):
        xx = (x + j) % 4
        return xx, (zh * 4 + xx, pi)

    def ringpeer(j):
        zz = (z8 + j) % 8
        return ((zz // 4) * 4 + x, y * 8 + (zz % 4) * 2 + k)

    zhpeer = ((1 - zh) * 4 + x, pi)

    small = [pltpu.make_async_copy(f_hbm, f, ssem.at[0]), pltpu.make_async_copy(lt_hbm, lt, ssem.at[1]),
             pltpu.make_async_copy(b_hbm, bv, ssem.at[2]), pltpu.make_async_copy(w_hbm, w_ref, ssem.at[3])]
    for c in small:
        c.start()

    def piece(i):
        s = pl.ds(pl.multiple_of(i * CH, CH), CH)
        return (pltpu.make_async_copy(e_hbm.at[s], e.at[s], dsem.at[0, i]),
                pltpu.make_async_copy(d_hbm.at[s], d.at[s], dsem.at[1, i]))

    for i in range(AHEAD):
        for c in piece(i):
            c.start()
    barrier = pltpu.get_barrier_semaphore()
    peers = [mate] + [ypeer(j)[1] for j in range(1, 4)] + [xpeer(j)[1] for j in range(1, 4)] + [ringpeer(j) for j in range(1, 8)]
    for dev in peers:
        pl.semaphore_signal(barrier, inc=1, device_id=dev, device_id_type=MESH)
    f3[64:128, :] = jnp.zeros((64, 1024), BF)
    row = lax.broadcasted_iota(jnp.int32, (16, 1024), 0)
    f3[64:80, :] = jnp.where(row < 3, 1.0, 0.0).astype(BF)
    v[...] = jnp.zeros_like(v)
    gall[pl.ds(0, R), :] = jnp.zeros((R, 1024), BF)
    for c in small:
        c.wait()
    for t in range(8):
        h, m, l = split3(f[t].astype(F32) * LOG2E)
        sl = slice(t * 128, (t + 1) * 128)
        f3[0:64, sl] = h
        f3[128:192, sl] = m
        f3[192:256, sl] = l
        f2[:, sl] = f[t]
    wneg = [-math.log(2.0) * w_ref[t] for t in range(8)]

    def ydot(j, yy):
        cs = pl.ds(pl.multiple_of(j * R, R), R)
        l = lt[:, cs]
        h, m, lo = split3(jnp.log2(bv[:, cs] * (0.5 * LOG2E)))
        row = lax.broadcasted_iota(jnp.int32, (16, R), 0)
        extra = jnp.where(row == 0, h.astype(F32), jnp.where(row == 1, m.astype(F32), jnp.where(row == 2, lo.astype(F32), 0.0))).astype(BF)
        l3 = jnp.concatenate([l, extra, jnp.zeros((48, R), BF), l, l], axis=0)
        yy[...] = lax.dot_general(l3, f3[...], (((0,), (0,)), ((), ())), preferred_element_type=F32)

    def elem(j, yy):
        acc = None
        for q in range(R // RB):
            r = pl.multiple_of(j * R + q * RB, RB)
            rl = slice(q * RB, (q + 1) * RB)
            dd_ = d[pl.ds(r, RB), :]
            et[q * RB * 8:(q + 1) * RB * 8, :] = e[pl.ds(r, RB)].astype(F32).reshape(RB * 8, 128)
            sums = []
            for o in range(0, RB, 8):
                rates, wt, hz = [], [], None
                for t in range(8):
                    rt = jnp.exp2(yy[q * RB + o:q * RB + o + 8, t * 128:(t + 1) * 128])
                    hz = -rt if t == 0 else hz - rt
                    s = jnp.exp2(hz)
                    a = jnp.where(t < dd_[o:o + 8], et[pl.ds((q * RB + o) * 8 + t, 8, stride=8), :], 0.0) * wneg[t]
                    rates.append(rt)
                    wt.append(a * s)
                g = None
                for t in range(7, -1, -1):
                    g = wt[t] if g is None else g + wt[t]
                    rates[t] = rates[t] * g
                sums.append(rates)
                acc = g if acc is None else acc + g
            for t in range(8):
                gall[pl.ds(r, RB), t * 128:(t + 1) * 128] = jnp.concatenate([rates[t] for rates in sums], axis=0).astype(BF)
        v[...] += acc

    def ddot(j):
        cs = pl.ds(pl.multiple_of(j * R, R), R)
        lg[:, cs] = lax.dot_general(f2[...], gall[cs, :], (((1,), (1,)), ((), ())), preferred_element_type=F32)

    def rc(src, dst, ss, rs_, dev):
        return pltpu.make_async_remote_copy(src, dst, ss, rs_, device_id=dev, device_id_type=MESH)

    mine = pl.multiple_of(k * 32, 32)
    other = pl.multiple_of(32 - k * 32, 32)
    rows = pl.ds(pl.multiple_of(mine + y * 8, 8), 8)

    def cols(i):
        lo = 0 if i == 0 else ENDS[i - 1]
        return pl.ds(lo, ENDS[i] - lo)

    def ccopy(i):
        return rc(lg.at[pl.ds(other, 32), cols(i)], cbuf.at[:, cols(i)], s_c.at[i], r_c.at[i], mate)

    def ycopy(i, j):
        yy, dev = ypeer(j)
        return rc(cbuf.at[pl.ds(pl.multiple_of(yy * 8, 8), 8), cols(i)], ybuf.at[j, :, cols(i)], s_y.at[i, j], r_y.at[i, j], dev)

    def zcopy(i, j):
        p = zbuf.at[z, :, cols(i)]
        return rc(p, p, s_z.at[i, j], r_z.at[i, j], zpeer(j))

    def acopy(i, j):
        p = lo_ref.at[rows, cols(i)]
        return rc(p, p, s_a.at[i, j], r_a.at[i, j], ypeer(j)[1])

    def dcopy(i):
        half = lo_ref.at[pl.ds(mine, 32), cols(i)]
        return rc(half, half, s_d.at[i], r_d.at[i], mate)

    def core_out(i):
        ccopy(i).start()

    def y_out(i):
        ccopy(i).wait_recv()
        cbuf[:, cols(i)] = cbuf[:, cols(i)] + lg[pl.ds(mine, 32), cols(i)]
        for j in (2, 1, 3):
            ycopy(i, j).start()

    def z_out(i):
        a = cbuf[pl.ds(pl.multiple_of(y * 8, 8), 8), cols(i)]
        for j in range(1, 4):
            ycopy(i, j).wait_recv()
            a = a + ybuf[j, :, cols(i)]
        zbuf[z, :, cols(i)] = a
        for j in range(1, 4):
            zcopy(i, j).start()

    def a_out(i):
        for j in range(1, 4):
            zcopy(i, j).wait_recv()
        a = (zbuf[0, :, cols(i)] + zbuf[1, :, cols(i)]) + (zbuf[2, :, cols(i)] + zbuf[3, :, cols(i)])
        lo_ref[rows, cols(i)] = a * scale_l
        for j in (2, 1, 3):
            acopy(i, j).start()

    def d_out(i):
        for j in range(1, 4):
            acopy(i, j).wait_recv()
        dcopy(i).start()

    def fcopy(j):
        xx, dev = xpeer(j)
        return rc(fp.at[:, xx], fx.at[j], s_f.at[j], r_f.at[j], dev)

    fzcopy = rc(fz.at[1 - zh], fz.at[2], s_f.at[0], r_f.at[0], zhpeer)
    vcopy = rc(v, vc, s_v.at[0], r_v.at[0], mate)

    def vycopy(j):
        return rc(vy.at[y], vy.at[y], s_v.at[j], r_v.at[j], ypeer(j)[1])

    def vxcopy(j):
        return rc(vx.at[x], vx.at[x], s_v.at[3 + j], r_v.at[3 + j], xpeer(j)[1])

    def vzcopy(j):
        return rc(vz.at[z8], vz.at[z8], s_v.at[6 + j], r_v.at[6 + j], ringpeer(j))

    at = {2: [(core_out, 0)], 3: [(y_out, 0)], 4: [(core_out, 1)], 5: [(y_out, 1)], 6: [(core_out, 2), (z_out, 0)], 7: [(y_out, 2)]}

    ydot(0, ya)

    def body(n, _):
        @pl.when(n < NB // 2 - AHEAD)
        def _():
            for c in piece(n + AHEAD):
                c.start()

        for c in piece(n):
            c.wait()
        j = 2 * n
        ydot(j + 1, yb)
        elem(j, ya)
        ddot(jnp.maximum(j - 1, 0))
        ydot(jnp.minimum(j + 2, NB - 1), ya)
        elem(j + 1, yb)
        ddot(j)

        @pl.when(n == 2)
        def _():
            pl.semaphore_wait(barrier, len(peers))

        for when_, todo in at.items():
            @pl.when(n == when_)
            def _():
                for step, i in todo:
                    step(i)

        return 0

    lax.fori_loop(0, NB // 2, body, 0)
    ddot(NB - 1)
    core_out(3)
    vcopy.start()
    z_out(1)
    y_out(3)
    vcopy.wait_recv()
    vy[y] = v[...] + vc[...]
    for j in (2, 1, 3):
        vycopy(j).start()
    for t in range(0, 8, 2):
        part = lax.dot_general(lt[...], gall[:, t * 128:(t + 2) * 128], (((1,), (0,)), ((), ())), preferred_element_type=F32)
        fp[:, :, :, t * 128:(t + 2) * 128] = part.reshape(2, 4, 8, 256)
    for j in (2, 1, 3):
        fcopy(j).start()
    z_out(2)
    for j in range(1, 4):
        vycopy(j).wait_recv()
    vx[x] = (vy[0] + vy[1]) + (vy[2] + vy[3])
    for j in (2, 1, 3):
        vxcopy(j).start()
    z_out(3)
    a_out(0)
    a_out(1)
    for j in range(1, 4):
        vxcopy(j).wait_recv()
    vz[z8] = (vx[0] + vx[1]) + (vx[2] + vx[3])
    for j in (4, 3, 5, 2, 6, 1, 7):
        vzcopy(j).start()
    a = fp[:, x]
    for j in range(1, 4):
        fcopy(j).wait_recv()
        a = a + fx[j]
    fz[0:2] = a
    fzcopy.start()
    a_out(2)
    d_out(0)
    a_out(3)
    d_out(1)
    for j in range(1, 8):
        vzcopy(j).wait_recv()
    a = ((vz[0] + vz[1]) + (vz[2] + vz[3])) + ((vz[4] + vz[5]) + (vz[6] + vz[7]))
    vo_ref[...] = jnp.sum(a, axis=(0, 1), keepdims=True) * scale_v
    fzcopy.wait_recv()
    a = (fz[zh] + fz[2]) * scale_f
    for t in range(8):
        fo_ref[t] = a[:, t * 128:(t + 1) * 128]
    d_out(2)
    d_out(3)
    vcopy.wait_send()
    fzcopy.wait_send()
    for j in range(1, 4):
        vycopy(j).wait_send()
        vxcopy(j).wait_send()
        fcopy(j).wait_send()
    for j in range(1, 8):
        vzcopy(j).wait_send()
    for i in range(4):
        ccopy(i).wait_send()
        for j in range(1, 4):
            ycopy(i, j).wait_send()
            zcopy(i, j).wait_send()
            acopy(i, j).wait_send()
        dcopy(i).wait_recv()
        dcopy(i).wait_send()


def finish(lo, fo, vo, lo_ref, fo_ref, vo_ref, sem):
    copies = [pltpu.make_async_copy(lo.at[pl.ds(8 * i, 8)], lo_ref.at[pl.ds(8 * i, 8)], sem.at[i]) for i in range(8)]
    copies += [pltpu.make_async_copy(fo, fo_ref, sem.at[8]), pltpu.make_async_copy(vo, vo_ref, sem.at[9])]
    for c in copies:
        c.start()
    for c in copies:
        c.wait()


def per_device(exposures, defaults, base_rate, loadings, factors, weights):
    paths = lax.axis_size("path") * factors.shape[2]
    cptys = lax.axis_size("cpty") * loadings.shape[0]
    scales = 1.0 / paths, factors.shape[1] / cptys, -1.0 / (math.log(2.0) * cptys * paths)
    A = pl.BlockSpec(memory_space=pl.ANY)
    H = pl.BlockSpec(memory_space=pltpu.HBM)
    D = pltpu.SemaphoreType.DMA
    shapes = [jax.ShapeDtypeStruct((64, CT), F32), jax.ShapeDtypeStruct((8, 8, 128), F32), jax.ShapeDtypeStruct((1, 1), F32)]
    lo, fo, vo = pl.pallas_call(
        functools.partial(kernel, *scales),
        in_specs=[H] * 6,
        out_specs=[pl.BlockSpec(memory_space=V)] * 3,
        out_shape=shapes,
        scratch_shapes=[
            V((CT, 8, 128), BF), V((CT, 128), jnp.int32), V((1, CT), F32), V((64, CT), BF), V((8, 64, 128), BF),
            V((256, 1024), BF), V((64, 1024), BF), V((R, 1024), F32), V((R, 1024), F32), V((R * 8, 128), F32), V((CT, 1024), BF),
            V((2, 4, 8, 1024), F32), V((64, CT), F32), V((8, 128), F32),
            V((32, CT), F32), V((4, 8, CT), F32), V((4, 8, CT), F32),
            V((4, 2, 8, 1024), F32), V((3, 8, 1024), F32), V((8, 128), F32), V((4, 8, 128), F32), V((4, 8, 128), F32), V((8, 8, 128), F32),
            pltpu.SMEM((8,), F32), D((2, NB // 2)), D((4,)), D((4,)), D((4,)), D((4, 4)), D((4, 4)), D((4, 4)), D((4, 4)), D((4, 4)), D((4, 4)), D((4,)), D((4,)),
            D((4,)), D((4,)), D((16,)), D((16,))],
        compiler_params=pltpu.CompilerParams(collective_id=0, has_side_effects=True, vmem_limit_bytes=44 << 20),
        name="adjoint",
    )(*(pltpu.with_memory_space_constraint(a, pltpu.HBM) for a in (exposures, defaults, base_rate[None, :], loadings.T, factors, weights)))
    lo, fo, vo = (pltpu.with_memory_space_constraint(a, pltpu.VMEM) for a in (lo, fo, vo))
    lo, fo, vo = pl.pallas_call(
        finish,
        in_specs=[A, A, A],
        out_specs=[H, H, H],
        out_shape=shapes,
        scratch_shapes=[D((10,))],
        name="finish",
    )(lo, fo, vo)
    return vo[0, 0], lo.T, fo


def solution(mesh):
    in_specs = (P("cpty", None, "path"), P("cpty", "path"), P("cpty"), P("cpty", None), P(None, None, "path"), P())
    out_specs = (P(), P("cpty", None), P(None, "cpty", "path"))
    return jax.shard_map(per_device, mesh=mesh, in_specs=in_specs, out_specs=out_specs, check_vma=False)
```

```python
import functools
import math

import jax
import jax.numpy as jnp
from jax import lax
from jax.experimental import pallas as pl
from jax.experimental.pallas import tpu as pltpu
from jax.sharding import PartitionSpec as P

LOG2E = 1.4426950408889634
F32, BF = jnp.float32, jnp.bfloat16
MESH = pl.DeviceIdType.MESH
V = pltpu.VMEM


def split3(v):
    h = v.astype(BF)
    r = v - h.astype(F32)
    m = r.astype(BF)
    return h, m, (r - m.astype(F32)).astype(BF)


CT = 4096
R, RB = 256, 16
NB = CT // R
CH = 2 * R
AHEAD = 1
ENDS = (1280, 2304, 3328, 4096)


def kernel(scale_l, scale_f, scale_v, e_hbm, d_hbm, b_hbm, lt_hbm, f_hbm, w_hbm, lo_ref, fo_ref, vo_ref,
           e, d, bv, lt, f, f3, f2, ya, yb, et, gall, fp, lg, v, cbuf, ybuf, zbuf, fx, fz, vc, vy, vx, vz,
           w_ref, dsem, ssem, s_c, r_c, s_y, r_y, s_z, r_z, s_a, r_a, s_d, r_d, s_f, r_f, s_v, r_v):
    ci, pi = lax.axis_index("cpty"), lax.axis_index("path")
    zh, x = ci // 4, ci % 4
    y, z, k = pi // 8, (pi // 2) % 4, pi % 2
    z8 = zh * 4 + z
    mate = (ci, pi - k + (1 - k))

    def ypeer(j):
        yy = (y + j) % 4
        return yy, (ci, yy * 8 + z * 2 + k)

    def zpeer(j):
        return (ci, y * 8 + ((z + j) % 4) * 2 + k)

    def xpeer(j):
        xx = (x + j) % 4
        return xx, (zh * 4 + xx, pi)

    def ringpeer(j):
        zz = (z8 + j) % 8
        return ((zz // 4) * 4 + x, y * 8 + (zz % 4) * 2 + k)

    zhpeer = ((1 - zh) * 4 + x, pi)

    first, rest = pl.ds(0, CH), pl.ds(CH, CT - CH)
    late = pltpu.make_async_copy(lt_hbm.at[:, rest], lt.at[:, rest], ssem.at[4])
    small = [pltpu.make_async_copy(f_hbm, f, ssem.at[0]), pltpu.make_async_copy(lt_hbm.at[:, first], lt.at[:, first], ssem.at[1]),
             pltpu.make_async_copy(b_hbm, bv, ssem.at[2]), pltpu.make_async_copy(w_hbm, w_ref, ssem.at[3])]
    for c in small:
        c.start()

    def piece(i):
        s = pl.ds(pl.multiple_of(i * CH, CH), CH)
        return (pltpu.make_async_copy(e_hbm.at[s], e.at[s], dsem.at[0, i]),
                pltpu.make_async_copy(d_hbm.at[s], d.at[s], dsem.at[1, i]))

    for i in range(AHEAD):
        for c in piece(i):
            c.start()
    late.start()
    barrier = pltpu.get_barrier_semaphore()
    peers = [mate] + [ypeer(j)[1] for j in range(1, 4)] + [xpeer(j)[1] for j in range(1, 4)] + [ringpeer(j) for j in range(1, 8)]
    for dev in peers:
        pl.semaphore_signal(barrier, inc=1, device_id=dev, device_id_type=MESH)
    f3[64:128, :] = jnp.zeros((64, 1024), BF)
    row = lax.broadcasted_iota(jnp.int32, (16, 1024), 0)
    f3[64:80, :] = jnp.where(row < 3, 1.0, 0.0).astype(BF)
    v[...] = jnp.zeros_like(v)
    small[0].wait()
    for t in range(8):
        h, m, l = split3(f[t].astype(F32) * LOG2E)
        sl = slice(t * 128, (t + 1) * 128)
        f3[0:64, sl] = h
        f3[128:192, sl] = m
        f3[192:256, sl] = l
        f2[:, sl] = f[t]
    for c in small[1:]:
        c.wait()
    wneg = [-math.log(2.0) * w_ref[t] for t in range(8)]

    def ydot(j, yy):
        cs = pl.ds(pl.multiple_of(j * R, R), R)
        l = lt[:, cs]
        h, m, lo = split3(jnp.log2(bv[:, cs] * (0.5 * LOG2E)))
        row = lax.broadcasted_iota(jnp.int32, (16, R), 0)
        extra = jnp.where(row == 0, h.astype(F32), jnp.where(row == 1, m.astype(F32), jnp.where(row == 2, lo.astype(F32), 0.0))).astype(BF)
        l3 = jnp.concatenate([l, extra, jnp.zeros((48, R), BF), l, l], axis=0)
        yy[...] = lax.dot_general(l3, f3[...], (((0,), (0,)), ((), ())), preferred_element_type=F32)

    def elem(j, yy):
        acc = None
        for q in range(R // RB):
            r = pl.multiple_of(j * R + q * RB, RB)
            rl = slice(q * RB, (q + 1) * RB)
            dd_ = d[pl.ds(r, RB), :]
            et[q * RB * 8:(q + 1) * RB * 8, :] = e[pl.ds(r, RB)].astype(F32).reshape(RB * 8, 128)
            sums = []
            for o in range(0, RB, 8):
                rates, wt, hz = [], [], None
                for t in range(8):
                    rt = jnp.exp2(yy[q * RB + o:q * RB + o + 8, t * 128:(t + 1) * 128])
                    hz = -rt if t == 0 else hz - rt
                    s = jnp.exp2(hz)
                    a = jnp.where(t < dd_[o:o + 8], et[pl.ds((q * RB + o) * 8 + t, 8, stride=8), :], 0.0) * wneg[t]
                    rates.append(rt)
                    wt.append(a * s)
                g = None
                for t in range(7, -1, -1):
                    g = wt[t] if g is None else g + wt[t]
                    rates[t] = rates[t] * g
                sums.append(rates)
                acc = g if acc is None else acc + g
            for t in range(8):
                gall[pl.ds(r, RB), t * 128:(t + 1) * 128] = jnp.concatenate([rates[t] for rates in sums], axis=0).astype(BF)
        v[...] += acc

    def ddot(j):
        cs = pl.ds(pl.multiple_of(j * R, R), R)
        lg[:, cs] = lax.dot_general(f2[...], gall[cs, :], (((1,), (1,)), ((), ())), preferred_element_type=F32)

    def rc(src, dst, ss, rs_, dev):
        return pltpu.make_async_remote_copy(src, dst, ss, rs_, device_id=dev, device_id_type=MESH)

    mine = pl.multiple_of(k * 32, 32)
    other = pl.multiple_of(32 - k * 32, 32)
    rows = pl.ds(pl.multiple_of(mine + y * 8, 8), 8)

    def cols(i):
        lo = 0 if i == 0 else ENDS[i - 1]
        return pl.ds(lo, ENDS[i] - lo)

    def ccopy(i):
        return rc(lg.at[pl.ds(other, 32), cols(i)], cbuf.at[:, cols(i)], s_c.at[i], r_c.at[i], mate)

    def ycopy(i, j):
        yy, dev = ypeer(j)
        return rc(cbuf.at[pl.ds(pl.multiple_of(yy * 8, 8), 8), cols(i)], ybuf.at[j, :, cols(i)], s_y.at[i, j], r_y.at[i, j], dev)

    def zcopy(i, j):
        p = zbuf.at[z, :, cols(i)]
        return rc(p, p, s_z.at[i, j], r_z.at[i, j], zpeer(j))

    def acopy(i, j):
        p = lo_ref.at[rows, cols(i)]
        return rc(p, p, s_a.at[i, j], r_a.at[i, j], ypeer(j)[1])

    def dcopy(i):
        half = lo_ref.at[pl.ds(mine, 32), cols(i)]
        return rc(half, half, s_d.at[i], r_d.at[i], mate)

    def core_out(i):
        ccopy(i).start()

    def y_out(i):
        ccopy(i).wait_recv()
        cbuf[:, cols(i)] = cbuf[:, cols(i)] + lg[pl.ds(mine, 32), cols(i)]
        for j in (2, 1, 3):
            ycopy(i, j).start()

    def z_out(i):
        a = cbuf[pl.ds(pl.multiple_of(y * 8, 8), 8), cols(i)]
        for j in range(1, 4):
            ycopy(i, j).wait_recv()
            a = a + ybuf[j, :, cols(i)]
        zbuf[z, :, cols(i)] = a
        for j in range(1, 4):
            zcopy(i, j).start()

    def a_out(i):
        for j in range(1, 4):
            zcopy(i, j).wait_recv()
        a = (zbuf[0, :, cols(i)] + zbuf[1, :, cols(i)]) + (zbuf[2, :, cols(i)] + zbuf[3, :, cols(i)])
        lo_ref[rows, cols(i)] = a * scale_l
        for j in (2, 1, 3):
            acopy(i, j).start()

    def d_out(i):
        for j in range(1, 4):
            acopy(i, j).wait_recv()
        dcopy(i).start()

    def fcopy(j):
        xx, dev = xpeer(j)
        return rc(fp.at[:, xx], fx.at[j], s_f.at[j], r_f.at[j], dev)

    fzcopy = rc(fz.at[1 - zh], fz.at[2], s_f.at[0], r_f.at[0], zhpeer)
    vcopy = rc(v, vc, s_v.at[0], r_v.at[0], mate)

    def vycopy(j):
        return rc(vy.at[y], vy.at[y], s_v.at[j], r_v.at[j], ypeer(j)[1])

    def vxcopy(j):
        return rc(vx.at[x], vx.at[x], s_v.at[3 + j], r_v.at[3 + j], xpeer(j)[1])

    def vzcopy(j):
        return rc(vz.at[z8], vz.at[z8], s_v.at[6 + j], r_v.at[6 + j], ringpeer(j))

    at = {2: [(core_out, 0)], 3: [(y_out, 0)], 4: [(core_out, 1)], 5: [(y_out, 1)], 6: [(core_out, 2), (z_out, 0)], 7: [(y_out, 2)]}

    ydot(0, ya)
    late.wait()

    def body(n, _):
        @pl.when(n < NB // 2 - AHEAD)
        def _():
            for c in piece(n + AHEAD):
                c.start()

        for c in piece(n):
            c.wait()
        j = 2 * n
        ydot(j + 1, yb)
        elem(j, ya)
        ddot(jnp.maximum(j - 1, 0))
        ydot(jnp.minimum(j + 2, NB - 1), ya)
        elem(j + 1, yb)
        ddot(j)

        @pl.when(n == 2)
        def _():
            pl.semaphore_wait(barrier, len(peers))

        for when_, todo in at.items():
            @pl.when(n == when_)
            def _():
                for step, i in todo:
                    step(i)

        return 0

    lax.fori_loop(0, NB // 2, body, 0)
    ddot(NB - 1)
    core_out(3)
    vcopy.start()
    z_out(1)
    y_out(3)
    vcopy.wait_recv()
    vy[y] = v[...] + vc[...]
    for j in (2, 1, 3):
        vycopy(j).start()
    for t in range(0, 8, 2):
        part = lax.dot_general(lt[...], gall[:, t * 128:(t + 2) * 128], (((1,), (0,)), ((), ())), preferred_element_type=F32)
        fp[:, :, :, t * 128:(t + 2) * 128] = part.reshape(2, 4, 8, 256)
    for j in (2, 1, 3):
        fcopy(j).start()
    z_out(2)
    for j in range(1, 4):
        vycopy(j).wait_recv()
    vx[x] = (vy[0] + vy[1]) + (vy[2] + vy[3])
    for j in (2, 1, 3):
        vxcopy(j).start()
    z_out(3)
    a_out(0)
    a_out(1)
    for j in range(1, 4):
        vxcopy(j).wait_recv()
    vz[z8] = (vx[0] + vx[1]) + (vx[2] + vx[3])
    for j in (4, 3, 5, 2, 6, 1, 7):
        vzcopy(j).start()
    a = fp[:, x]
    for j in range(1, 4):
        fcopy(j).wait_recv()
        a = a + fx[j]
    fz[0:2] = a
    fzcopy.start()
    a_out(2)
    d_out(0)
    a_out(3)
    d_out(1)
    for j in range(1, 8):
        vzcopy(j).wait_recv()
    a = ((vz[0] + vz[1]) + (vz[2] + vz[3])) + ((vz[4] + vz[5]) + (vz[6] + vz[7]))
    vo_ref[...] = jnp.broadcast_to(jnp.sum(a, axis=(0, 1), keepdims=True) * scale_v, (8, 128))
    fzcopy.wait_recv()
    a = (fz[zh] + fz[2]) * scale_f
    for t in range(8):
        fo_ref[t] = a[:, t * 128:(t + 1) * 128]
    d_out(2)
    d_out(3)
    vcopy.wait_send()
    fzcopy.wait_send()
    for j in range(1, 4):
        vycopy(j).wait_send()
        vxcopy(j).wait_send()
        fcopy(j).wait_send()
    for j in range(1, 8):
        vzcopy(j).wait_send()
    for i in range(4):
        ccopy(i).wait_send()
        for j in range(1, 4):
            ycopy(i, j).wait_send()
            zcopy(i, j).wait_send()
            acopy(i, j).wait_send()
        dcopy(i).wait_recv()
        dcopy(i).wait_send()


def finish(lo, fo, vo, lo_ref, fo_ref, vo_ref, one, sem):
    one[...] = vo[0:1, 0:1]
    copies = [pltpu.make_async_copy(one, vo_ref, sem.at[9])]
    copies += [pltpu.make_async_copy(lo.at[pl.ds(8 * i, 8)], lo_ref.at[pl.ds(8 * i, 8)], sem.at[i]) for i in range(8)]
    copies += [pltpu.make_async_copy(fo, fo_ref, sem.at[8])]
    for c in copies:
        c.start()
    for c in copies:
        c.wait()


def per_device(exposures, defaults, base_rate, loadings, factors, weights):
    paths = lax.axis_size("path") * factors.shape[2]
    cptys = lax.axis_size("cpty") * loadings.shape[0]
    scales = 1.0 / paths, factors.shape[1] / cptys, -1.0 / (math.log(2.0) * cptys * paths)
    A = pl.BlockSpec(memory_space=pl.ANY)
    H = pl.BlockSpec(memory_space=pltpu.HBM)
    D = pltpu.SemaphoreType.DMA
    shapes = [jax.ShapeDtypeStruct((64, CT), F32), jax.ShapeDtypeStruct((8, 8, 128), F32), jax.ShapeDtypeStruct((1, 1), F32)]
    lo, fo, vo = pl.pallas_call(
        functools.partial(kernel, *scales),
        in_specs=[H] * 6,
        out_specs=[pl.BlockSpec(memory_space=V)] * 3,
        out_shape=shapes[:2] + [jax.ShapeDtypeStruct((8, 128), F32)],
        scratch_shapes=[
            V((CT, 8, 128), BF), V((CT, 128), jnp.int32), V((1, CT), F32), V((64, CT), BF), V((8, 64, 128), BF),
            V((256, 1024), BF), V((64, 1024), BF), V((R, 1024), F32), V((R, 1024), F32), V((R * 8, 128), F32), V((CT, 1024), BF),
            V((2, 4, 8, 1024), F32), V((64, CT), F32), V((8, 128), F32),
            V((32, CT), F32), V((4, 8, CT), F32), V((4, 8, CT), F32),
            V((4, 2, 8, 1024), F32), V((3, 8, 1024), F32), V((8, 128), F32), V((4, 8, 128), F32), V((4, 8, 128), F32), V((8, 8, 128), F32),
            pltpu.SMEM((8,), F32), D((2, NB // 2)), D((5,)), D((4,)), D((4,)), D((4, 4)), D((4, 4)), D((4, 4)), D((4, 4)), D((4, 4)), D((4, 4)), D((4,)), D((4,)),
            D((4,)), D((4,)), D((16,)), D((16,))],
        compiler_params=pltpu.CompilerParams(collective_id=0, has_side_effects=True, vmem_limit_bytes=44 << 20),
        name="adjoint",
    )(*(pltpu.with_memory_space_constraint(a, pltpu.HBM) for a in (exposures, defaults, base_rate[None, :], loadings.T, factors, weights)))
    lo, fo, vo = (pltpu.with_memory_space_constraint(a, pltpu.VMEM) for a in (lo, fo, vo))
    lo, fo, vo = pl.pallas_call(
        finish,
        in_specs=[A, A, pl.BlockSpec(memory_space=V)],
        out_specs=[H, H, H],
        out_shape=shapes,
        scratch_shapes=[V((1, 1), F32), D((10,))],
        name="finish",
    )(lo, fo, vo)
    return vo[0, 0], lo.T, fo


def solution(mesh):
    in_specs = (P("cpty", None, "path"), P("cpty", "path"), P("cpty"), P("cpty", None), P(None, None, "path"), P())
    out_specs = (P(), P("cpty", None), P(None, "cpty", "path"))
    return jax.shard_map(per_device, mesh=mesh, in_specs=in_specs, out_specs=out_specs, check_vma=False)
```

```python
import functools
import math

import jax
import jax.numpy as jnp
from jax import lax
from jax.experimental import pallas as pl
from jax.experimental.pallas import tpu as pltpu
from jax.sharding import PartitionSpec as P

LOG2E = 1.4426950408889634
F32, BF = jnp.float32, jnp.bfloat16
MESH = pl.DeviceIdType.MESH
V = pltpu.VMEM


def split3(v):
    h = v.astype(BF)
    r = v - h.astype(F32)
    m = r.astype(BF)
    return h, m, (r - m.astype(F32)).astype(BF)


CT = 4096
R, RB = 256, 16
NB = CT // R
CH = 2 * R
AHEAD = 1
ENDS = (1280, 2304, 3328, 4096)


def kernel(scale_l, scale_f, scale_v, e_hbm, d_hbm, b_hbm, lt_hbm, f_hbm, w_hbm, lo_ref, fo_ref, vo_ref,
           e, d, bv, lt, f, f3, f2, ya, yb, et, gall, fp, lg, v, cbuf, ybuf, zbuf, fx, fz, vc, vy, vx, vz,
           w_ref, dsem, ssem, s_c, r_c, s_y, r_y, s_z, r_z, s_a, r_a, s_d, r_d, s_f, r_f, s_v, r_v):
    ci, pi = lax.axis_index("cpty"), lax.axis_index("path")
    zh, x = ci // 4, ci % 4
    y, z, k = pi // 8, (pi // 2) % 4, pi % 2
    z8 = zh * 4 + z
    mate = (ci, pi - k + (1 - k))

    def ypeer(j):
        yy = (y + j) % 4
        return yy, (ci, yy * 8 + z * 2 + k)

    def zpeer(j):
        return (ci, y * 8 + ((z + j) % 4) * 2 + k)

    def xpeer(j):
        xx = (x + j) % 4
        return xx, (zh * 4 + xx, pi)

    def ringpeer(j):
        zz = (z8 + j) % 8
        return ((zz // 4) * 4 + x, y * 8 + (zz % 4) * 2 + k)

    zhpeer = ((1 - zh) * 4 + x, pi)

    first, rest = pl.ds(0, CH), pl.ds(CH, CT - CH)
    late = pltpu.make_async_copy(lt_hbm.at[:, rest], lt.at[:, rest], ssem.at[4])
    small = [pltpu.make_async_copy(f_hbm, f, ssem.at[0]), pltpu.make_async_copy(lt_hbm.at[:, first], lt.at[:, first], ssem.at[1]),
             pltpu.make_async_copy(b_hbm, bv, ssem.at[2]), pltpu.make_async_copy(w_hbm, w_ref, ssem.at[3])]
    for c in small:
        c.start()

    def piece(i):
        s = pl.ds(pl.multiple_of(i * CH, CH), CH)
        return (pltpu.make_async_copy(e_hbm.at[s], e.at[s], dsem.at[0, i]),
                pltpu.make_async_copy(d_hbm.at[s], d.at[s], dsem.at[1, i]))

    for i in range(AHEAD):
        for c in piece(i):
            c.start()
    late.start()
    barrier = pltpu.get_barrier_semaphore()
    peers = [mate] + [ypeer(j)[1] for j in range(1, 4)] + [xpeer(j)[1] for j in range(1, 4)] + [ringpeer(j) for j in range(1, 8)]
    for dev in peers:
        pl.semaphore_signal(barrier, inc=1, device_id=dev, device_id_type=MESH)
    f3[64:128, :] = jnp.zeros((64, 1024), BF)
    row = lax.broadcasted_iota(jnp.int32, (16, 1024), 0)
    f3[64:80, :] = jnp.where(row < 3, 1.0, 0.0).astype(BF)
    v[...] = jnp.zeros_like(v)
    small[0].wait()
    for t in range(8):
        h, m, l = split3(f[t].astype(F32) * LOG2E)
        sl = slice(t * 128, (t + 1) * 128)
        f3[0:64, sl] = h
        f3[128:192, sl] = m
        f3[192:256, sl] = l
        f2[:, sl] = f[t]
    for c in small[1:]:
        c.wait()
    wneg = [-math.log(2.0) * w_ref[t] for t in range(8)]

    def ydot(j, yy):
        cs = pl.ds(pl.multiple_of(j * R, R), R)
        l = lt[:, cs]
        h, m, lo = split3(jnp.log2(bv[:, cs] * (0.5 * LOG2E)))
        row = lax.broadcasted_iota(jnp.int32, (16, R), 0)
        extra = jnp.where(row == 0, h.astype(F32), jnp.where(row == 1, m.astype(F32), jnp.where(row == 2, lo.astype(F32), 0.0))).astype(BF)
        l3 = jnp.concatenate([l, extra, jnp.zeros((48, R), BF), l, l], axis=0)
        yy[...] = lax.dot_general(l3, f3[...], (((0,), (0,)), ((), ())), preferred_element_type=F32)

    def elem(j, yy):
        acc = None
        for q in range(R // RB):
            r = pl.multiple_of(j * R + q * RB, RB)
            rl = slice(q * RB, (q + 1) * RB)
            dd_ = d[pl.ds(r, RB), :]
            et[q * RB * 8:(q + 1) * RB * 8, :] = e[pl.ds(r, RB)].astype(F32).reshape(RB * 8, 128)
            sums = []
            for o in range(0, RB, 8):
                rates, wt, hz = [], [], None
                for t in range(8):
                    rt = jnp.exp2(yy[q * RB + o:q * RB + o + 8, t * 128:(t + 1) * 128])
                    hz = -rt if t == 0 else hz - rt
                    s = jnp.exp2(hz)
                    a = jnp.where(t < dd_[o:o + 8], et[pl.ds((q * RB + o) * 8 + t, 8, stride=8), :], 0.0) * wneg[t]
                    rates.append(rt)
                    wt.append(a * s)
                g = None
                for t in range(7, -1, -1):
                    g = wt[t] if g is None else g + wt[t]
                    rates[t] = rates[t] * g
                sums.append(rates)
                acc = g if acc is None else acc + g
            for t in range(8):
                gall[pl.ds(r, RB), t * 128:(t + 1) * 128] = jnp.concatenate([rates[t] for rates in sums], axis=0).astype(BF)
        v[...] += acc

    def ddot(j):
        cs = pl.ds(pl.multiple_of(j * R, R), R)
        lg[:, cs] = lax.dot_general(f2[...], gall[cs, :], (((1,), (1,)), ((), ())), preferred_element_type=F32)

    def rc(src, dst, ss, rs_, dev):
        return pltpu.make_async_remote_copy(src, dst, ss, rs_, device_id=dev, device_id_type=MESH)

    mine = pl.multiple_of(k * 32, 32)
    other = pl.multiple_of(32 - k * 32, 32)
    rows = pl.ds(pl.multiple_of(mine + y * 8, 8), 8)

    def cols(i):
        lo = 0 if i == 0 else ENDS[i - 1]
        return pl.ds(lo, ENDS[i] - lo)

    def ccopy(i):
        return rc(lg.at[pl.ds(other, 32), cols(i)], cbuf.at[:, cols(i)], s_c.at[i], r_c.at[i], mate)

    def ycopy(i, j):
        yy, dev = ypeer(j)
        return rc(cbuf.at[pl.ds(pl.multiple_of(yy * 8, 8), 8), cols(i)], ybuf.at[j, :, cols(i)], s_y.at[i, j], r_y.at[i, j], dev)

    def zcopy(i, j):
        p = zbuf.at[z, :, cols(i)]
        return rc(p, p, s_z.at[i, j], r_z.at[i, j], zpeer(j))

    def acopy(i, j):
        p = lo_ref.at[rows, cols(i)]
        return rc(p, p, s_a.at[i, j], r_a.at[i, j], ypeer(j)[1])

    def dcopy(i):
        half = lo_ref.at[pl.ds(mine, 32), cols(i)]
        return rc(half, half, s_d.at[i], r_d.at[i], mate)

    def core_out(i):
        ccopy(i).start()

    def y_out(i):
        ccopy(i).wait_recv()
        cbuf[:, cols(i)] = cbuf[:, cols(i)] + lg[pl.ds(mine, 32), cols(i)]
        for j in (2, 1, 3):
            ycopy(i, j).start()

    def z_out(i):
        a = cbuf[pl.ds(pl.multiple_of(y * 8, 8), 8), cols(i)]
        for j in range(1, 4):
            ycopy(i, j).wait_recv()
            a = a + ybuf[j, :, cols(i)]
        zbuf[z, :, cols(i)] = a
        for j in range(1, 4):
            zcopy(i, j).start()

    def a_out(i):
        for j in range(1, 4):
            zcopy(i, j).wait_recv()
        a = (zbuf[0, :, cols(i)] + zbuf[1, :, cols(i)]) + (zbuf[2, :, cols(i)] + zbuf[3, :, cols(i)])
        lo_ref[rows, cols(i)] = a * scale_l
        for j in (2, 1, 3):
            acopy(i, j).start()

    def d_out(i):
        for j in range(1, 4):
            acopy(i, j).wait_recv()
        dcopy(i).start()

    def fcopy(j):
        xx, dev = xpeer(j)
        return rc(fp.at[:, xx], fx.at[j], s_f.at[j], r_f.at[j], dev)

    fzcopy = rc(fz.at[1 - zh], fz.at[2], s_f.at[0], r_f.at[0], zhpeer)
    vcopy = rc(v, vc, s_v.at[0], r_v.at[0], mate)

    def vycopy(j):
        return rc(vy.at[y], vy.at[y], s_v.at[j], r_v.at[j], ypeer(j)[1])

    def vxcopy(j):
        return rc(vx.at[x], vx.at[x], s_v.at[3 + j], r_v.at[3 + j], xpeer(j)[1])

    def vzcopy(j):
        return rc(vz.at[z8], vz.at[z8], s_v.at[6 + j], r_v.at[6 + j], ringpeer(j))

    at = {2: [(core_out, 0)], 3: [(y_out, 0)], 4: [(core_out, 1)], 5: [(y_out, 1)], 6: [(core_out, 2), (z_out, 0)], 7: [(y_out, 2)]}

    ydot(0, ya)
    late.wait()

    def body(n, _):
        @pl.when(n < NB // 2 - AHEAD)
        def _():
            for c in piece(n + AHEAD):
                c.start()

        for c in piece(n):
            c.wait()
        j = 2 * n
        ydot(j + 1, yb)
        elem(j, ya)
        ddot(jnp.maximum(j - 1, 0))
        ydot(jnp.minimum(j + 2, NB - 1), ya)
        elem(j + 1, yb)
        ddot(j)

        @pl.when(n == 2)
        def _():
            pl.semaphore_wait(barrier, len(peers))

        for when_, todo in at.items():
            @pl.when(n == when_)
            def _():
                for step, i in todo:
                    step(i)

        return 0

    lax.fori_loop(0, NB // 2, body, 0)
    ddot(NB - 1)
    core_out(3)
    vcopy.start()
    z_out(1)
    y_out(3)
    vcopy.wait_recv()
    vy[y] = v[...] + vc[...]
    for j in (2, 1, 3):
        vycopy(j).start()
    for t in range(0, 8, 2):
        part = lax.dot_general(lt[...], gall[:, t * 128:(t + 2) * 128], (((1,), (0,)), ((), ())), preferred_element_type=F32)
        fp[:, :, :, t * 128:(t + 2) * 128] = part.reshape(2, 4, 8, 256)
    for j in (2, 1, 3):
        fcopy(j).start()
    z_out(2)
    for j in range(1, 4):
        vycopy(j).wait_recv()
    vx[x] = (vy[0] + vy[1]) + (vy[2] + vy[3])
    for j in (2, 1, 3):
        vxcopy(j).start()
    z_out(3)
    a_out(0)
    a_out(1)
    for j in range(1, 4):
        vxcopy(j).wait_recv()
    vz[z8] = (vx[0] + vx[1]) + (vx[2] + vx[3])
    for j in (4, 3, 5, 2, 6, 1, 7):
        vzcopy(j).start()
    a = fp[:, x]
    for j in range(1, 4):
        fcopy(j).wait_recv()
        a = a + fx[j]
    fz[0:2] = a
    fzcopy.start()
    a_out(2)
    d_out(0)
    a_out(3)
    d_out(1)
    vcopy.wait_send()
    for j in range(1, 4):
        vycopy(j).wait_send()
        vxcopy(j).wait_send()
        fcopy(j).wait_send()
    for i in range(4):
        ccopy(i).wait_send()
        for j in range(1, 4):
            ycopy(i, j).wait_send()
            zcopy(i, j).wait_send()
    for j in range(1, 8):
        vzcopy(j).wait()
    a = ((vz[0] + vz[1]) + (vz[2] + vz[3])) + ((vz[4] + vz[5]) + (vz[6] + vz[7]))
    vo_ref[...] = jnp.broadcast_to(jnp.sum(a, axis=(0, 1), keepdims=True) * scale_v, (8, 128))
    fzcopy.wait()
    a = (fz[zh] + fz[2]) * scale_f
    for t in range(8):
        fo_ref[t] = a[:, t * 128:(t + 1) * 128]
    d_out(2)
    d_out(3)
    for i in range(4):
        for j in range(1, 4):
            acopy(i, j).wait_send()
        dcopy(i).wait_recv()
        dcopy(i).wait_send()


def finish(lo, fo, vo, lo_ref, fo_ref, vo_ref, one, sem):
    one[...] = vo[0:1, 0:1]
    copies = [pltpu.make_async_copy(one, vo_ref, sem.at[9])]
    copies += [pltpu.make_async_copy(lo.at[pl.ds(8 * i, 8)], lo_ref.at[pl.ds(8 * i, 8)], sem.at[i]) for i in range(8)]
    copies += [pltpu.make_async_copy(fo, fo_ref, sem.at[8])]
    for c in copies:
        c.start()
    for c in copies:
        c.wait()


def per_device(exposures, defaults, base_rate, loadings, factors, weights):
    paths = lax.axis_size("path") * factors.shape[2]
    cptys = lax.axis_size("cpty") * loadings.shape[0]
    scales = 1.0 / paths, factors.shape[1] / cptys, -1.0 / (math.log(2.0) * cptys * paths)
    A = pl.BlockSpec(memory_space=pl.ANY)
    H = pl.BlockSpec(memory_space=pltpu.HBM)
    D = pltpu.SemaphoreType.DMA
    shapes = [jax.ShapeDtypeStruct((64, CT), F32), jax.ShapeDtypeStruct((8, 8, 128), F32), jax.ShapeDtypeStruct((1, 1), F32)]
    lo, fo, vo = pl.pallas_call(
        functools.partial(kernel, *scales),
        in_specs=[H] * 6,
        out_specs=[pl.BlockSpec(memory_space=V)] * 3,
        out_shape=shapes[:2] + [jax.ShapeDtypeStruct((8, 128), F32)],
        scratch_shapes=[
            V((CT, 8, 128), BF), V((CT, 128), jnp.int32), V((1, CT), F32), V((64, CT), BF), V((8, 64, 128), BF),
            V((256, 1024), BF), V((64, 1024), BF), V((R, 1024), F32), V((R, 1024), F32), V((R * 8, 128), F32), V((CT, 1024), BF),
            V((2, 4, 8, 1024), F32), V((64, CT), F32), V((8, 128), F32),
            V((32, CT), F32), V((4, 8, CT), F32), V((4, 8, CT), F32),
            V((4, 2, 8, 1024), F32), V((3, 8, 1024), F32), V((8, 128), F32), V((4, 8, 128), F32), V((4, 8, 128), F32), V((8, 8, 128), F32),
            pltpu.SMEM((8,), F32), D((2, NB // 2)), D((5,)), D((4,)), D((4,)), D((4, 4)), D((4, 4)), D((4, 4)), D((4, 4)), D((4, 4)), D((4, 4)), D((4,)), D((4,)),
            D((4,)), D((4,)), D((16,)), D((16,))],
        compiler_params=pltpu.CompilerParams(collective_id=0, has_side_effects=True, vmem_limit_bytes=44 << 20),
        name="adjoint",
    )(*(pltpu.with_memory_space_constraint(a, pltpu.HBM) for a in (exposures, defaults, base_rate[None, :], loadings.T, factors, weights)))
    lo, fo, vo = (pltpu.with_memory_space_constraint(a, pltpu.VMEM) for a in (lo, fo, vo))
    lo, fo, vo = pl.pallas_call(
        finish,
        in_specs=[A, A, pl.BlockSpec(memory_space=V)],
        out_specs=[H, H, H],
        out_shape=shapes,
        scratch_shapes=[V((1, 1), F32), D((10,))],
        name="finish",
    )(lo, fo, vo)
    return vo[0, 0], lo.T, fo


def solution(mesh):
    in_specs = (P("cpty", None, "path"), P("cpty", "path"), P("cpty"), P("cpty", None), P(None, None, "path"), P())
    out_specs = (P(), P("cpty", None), P(None, "cpty", "path"))
    return jax.shard_map(per_device, mesh=mesh, in_specs=in_specs, out_specs=out_specs, check_vma=False)
```
